512 devices in a mesh: gx: 8 (over z), gy: 8 (over y_lo, core), gz: 8 (over x, y_hi).
Axes of the slice: x: 4, y: 8 (y_hi: 2, y_lo: 4; y = y_hi * 4 + y_lo), z: 8, core: 2. Of those that a mesh axis runs over, the one named last changes fastest.
Arguments:
- node_irreps: bfloat16 [8, 8, 8, 16, 25, 128], P('gx', 'gy', 'gz'), may hold values from -5 to 11
- positions: float32 [8, 8, 8, 3, 16], P('gx', 'gy', 'gz'), may hold values from 0 to 6.8
- send_list: int32 [8, 8, 8, 8], P('gx', 'gy', 'gz'), may hold values from 0 to 15, as said below
- neighbours: int32 [8, 8, 8, 16, 32], P('gx', 'gy', 'gz'), may hold values from 0 to 231
- displacements: float32 [8, 8, 8, 3, 512], P('gx', 'gy', 'gz'), may hold values from -6 to 6
- order_zero: bfloat16 [640, 640], replicated, may hold values from -0.25 to 0.25
- order_one: bfloat16 [512, 1024], replicated, may hold values from -0.25 to 0.25
- order_two: bfloat16 [384, 768], replicated, may hold values from -0.3125 to 0.3125
- reciprocal_triples: int32 [1024, 3], replicated, may hold values from -6 to 6
- reciprocal_filter: float32 [1024, 128], replicated, may hold values from 0.1 to 1
- cotangent: float32 [8, 8, 8, 16, 128], P('gx', 'gy', 'gz'), may hold values from -5 to 11
Outputs:
- updated: bfloat16 [8, 8, 8, 16, 25, 128], P('gx', 'gy', 'gz')
- long_range: float32 [8, 8, 8, 16, 128], P('gx', 'gy', 'gz')
- charge_grad: float32 [8, 8, 8, 16, 128], P('gx', 'gy', 'gz')
- position_grad: float32 [8, 8, 8, 3, 16], P('gx', 'gy', 'gz')
The draws below stay inside these ranges and needn't reach their ends.
Inputs may be any that keep to these rules, and one draw needn't show every extreme that they name: `send_list`: entries of one block are distinct atoms of that block.
All inputs are finite; a program needn't handle non-finite values.
Results may differ from the reference program's by a relative error of at most 0.0023.
Values may be sent and summed in bfloat16 or wider, within the bound.
A program may use at most 64 MiB of HBM per device.

```python
import math
import jax
import jax.numpy as jnp
from jax import lax

CHANNEL_COUNT = 128
HARMONICS = 25
NEIGHBOURS = 32
WAVE_VECTORS = 1024
ATOMS_DEV = 16
GHOSTS = 8
BLOCKS_X = 8
BLOCKS_Y = 8
BLOCKS_Z = 8


def rising_field(key, trailing):
    noise_key, scale_key = jax.random.split(key, 2)
    shape = (BLOCKS_X, BLOCKS_Y, BLOCKS_Z, ATOMS_DEV) + trailing
    noise = jax.random.truncated_normal(noise_key, -5.0, 5.0, shape, jnp.float32)
    channel_scale = jnp.exp(jax.random.uniform(scale_key, (CHANNEL_COUNT,), jnp.float32, math.log(0.5), math.log(2.0)))
    rising = 1.0 + 2.0 * jnp.arange(BLOCKS_X, dtype=jnp.float32) / max(BLOCKS_X - 1, 1)
    offset = rising[:, None, None, None, None] * channel_scale
    return (noise, offset)


def draw_node_irreps(key, part):
    noise, offset = rising_field(jax.random.fold_in(key, 11), (HARMONICS, CHANNEL_COUNT))
    return noise.at[:, :, :, :, 0, :].add(offset).astype(jnp.bfloat16)


def draw_cotangent(key, part):
    noise, offset = rising_field(jax.random.fold_in(key, 23), (CHANNEL_COUNT,))
    return (noise + offset).astype(jnp.float32)


def draw_send_list(key, part):
    blocks_total = BLOCKS_X * BLOCKS_Y * BLOCKS_Z
    block_keys = jax.random.split(jax.random.fold_in(key, 37), blocks_total)
    chosen = jax.vmap(lambda one_key: jax.random.permutation(one_key, ATOMS_DEV)[:GHOSTS])(block_keys)
    return chosen.reshape(BLOCKS_X, BLOCKS_Y, BLOCKS_Z, GHOSTS).astype(jnp.int32)


def touch_ends(values, stream_key, low, top_value):
    longest = values.shape.index(max(values.shape))
    spots = []
    for shift in (0, 1):
        where = [jax.random.randint(jax.random.fold_in(stream_key, axis), (), 0, length) for axis, length in enumerate(values.shape)]
        where[longest] = (where[longest] + shift) % values.shape[longest]
        spots.append(tuple(where))
    return values.at[spots[0]].set(low).at[spots[1]].set(top_value)


def steps_of(own_key, dims, shards, smallest, top_value):
    def one(position, parts):
        draws = jax.random.uniform(jax.random.fold_in(jax.random.fold_in(own_key, 6), position), (parts,), jnp.float32, smallest / len(shards), top_value / len(shards))
        return jnp.repeat(jnp.exp(draws), dims[position] // parts).reshape((-1,) + (1,) * (len(dims) - position - 1))

    loudness = one(*shards[0])
    for cut in shards[1:]:
        loudness = loudness * one(*cut)
    return loudness


def centred(own_key, extent, deviation, most, kind=jnp.bfloat16):
    values = deviation * jax.random.normal(own_key, extent, jnp.float32)
    return jnp.clip(values, min=-most, max=most).astype(kind)


def setup_inputs(seed: int = 0) -> dict:
    seeds = jax.random.split(jax.random.key(seed), 12)
    return {
        "node_irreps": draw_node_irreps(jax.random.fold_in(seeds[11], 71), 0),
        "positions": jnp.clip(6.8 * jax.random.uniform(seeds[1], (BLOCKS_X, BLOCKS_Y, BLOCKS_Z, 3, ATOMS_DEV), jnp.float32) ** steps_of(seeds[1], (BLOCKS_X, BLOCKS_Y, BLOCKS_Z, 3, ATOMS_DEV), ((0, 8), (1, 8), (2, 8)), -0.2, 0.2), 0.0, 6.8),
        "send_list": draw_send_list(jax.random.fold_in(seeds[11], 71), 0),
        "neighbours": touch_ends(jax.random.randint(seeds[3], (BLOCKS_X, BLOCKS_Y, BLOCKS_Z, ATOMS_DEV, NEIGHBOURS), 0, ATOMS_DEV + 27 * GHOSTS), jax.random.fold_in(seeds[3], 1), 0, (ATOMS_DEV + 27 * GHOSTS) - 1).astype(jnp.int32),
        "displacements": jnp.clip(jax.random.uniform(seeds[4], (BLOCKS_X, BLOCKS_Y, BLOCKS_Z, 3, ATOMS_DEV * NEIGHBOURS), jnp.float32, -6.0, 6.0) * steps_of(seeds[4], (BLOCKS_X, BLOCKS_Y, BLOCKS_Z, 3, ATOMS_DEV * NEIGHBOURS), ((0, 8), (1, 8), (2, 8)), -0.4, 0.0), -6.0, 6.0),
        "order_zero": centred(seeds[5], (5 * CHANNEL_COUNT, 5 * CHANNEL_COUNT), (5 * CHANNEL_COUNT) ** -0.5, 0.25),
        "order_one": centred(seeds[6], (4 * CHANNEL_COUNT, 8 * CHANNEL_COUNT), (4 * CHANNEL_COUNT) ** -0.5, 0.25),
        "order_two": centred(seeds[7], (3 * CHANNEL_COUNT, 6 * CHANNEL_COUNT), (3 * CHANNEL_COUNT) ** -0.5, 0.3125),
        "reciprocal_triples": touch_ends(jax.random.randint(seeds[8], (WAVE_VECTORS, 3), -6, 7), jax.random.fold_in(seeds[8], 1), -6, 6).astype(jnp.int32),
        "reciprocal_filter": jnp.clip(jnp.exp(jax.random.uniform(seeds[9], (WAVE_VECTORS, CHANNEL_COUNT), jnp.float32, math.log(0.1), math.log(1.0))), 0.1, 1.0),
        "cotangent": draw_cotangent(jax.random.fold_in(seeds[11], 71), 0),
    }


highest = lax.Precision.HIGHEST
cell_length = 6.8
planar_floor = 0.25
radial_width = 64.0

def harmonic_slot(degree, signed_order):
    return degree * degree + degree + signed_order

def kept_rows(keep_all):
    layout = []
    for degree in range(5):
        for signed_order in range(-degree, degree + 1):
            if keep_all or abs(signed_order) <= 2:
                layout.append(harmonic_slot(degree, signed_order))
    return layout

def edge_messages(lookup_table, displacement, neighbour_index, order_zero, order_one, order_two, layout):
    atom_count = neighbour_index.shape[0]
    neighbour_count = neighbour_index.shape[1]
    flat_index = neighbour_index.reshape(-1)
    edge_count = flat_index.shape[0]
    feature_width = lookup_table.shape[2]
    source = lookup_table[flat_index]
    length_squared = lax.optimization_barrier(jnp.sum(displacement * displacement, axis=0))
    radial = jnp.exp(-length_squared / radial_width) / math.sqrt(neighbour_count)
    planar = jnp.sqrt(displacement[0] * displacement[0] + displacement[1] * displacement[1] + planar_floor)
    cos_one = displacement[0] / planar
    sin_one = displacement[1] / planar

    def neighbour_sum(values):
        weighted = values * radial[:, None, None]
        return lax.optimization_barrier(jnp.sum(weighted.reshape(atom_count, neighbour_count, values.shape[1], feature_width), axis=1))
    collected = {}
    zero_slots = [layout.index(harmonic_slot(degree, 0)) for degree in range(5)]
    zero_input = source[:, zero_slots, :].reshape(edge_count, 5 * feature_width)
    zero_output = jnp.dot(zero_input, order_zero, preferred_element_type=jnp.float32)
    summed_zero_part = neighbour_sum(zero_output.reshape(edge_count, 5, feature_width))
    for degree in range(5):
        collected[harmonic_slot(degree, 0)] = summed_zero_part[:, degree]
    rotations = ((1, cos_one, sin_one, order_one), (2, cos_one * cos_one - sin_one * sin_one, 2.0 * cos_one * sin_one, order_two))
    for harmonic_order, cosine, sine_term, weight_pair in rotations:
        degrees = list(range(harmonic_order, 5))
        count_of_rows = len(degrees)
        plus_slots = [layout.index(harmonic_slot(degree, harmonic_order)) for degree in degrees]
        minus_slots = [layout.index(harmonic_slot(degree, -harmonic_order)) for degree in degrees]
        plus_part = source[:, plus_slots, :].astype(jnp.float32)
        minus_part = source[:, minus_slots, :].astype(jnp.float32)
        cosine_wide = cosine[:, None, None]
        sine_wide = sine_term[:, None, None]
        turned_plus = (cosine_wide * plus_part + sine_wide * minus_part).astype(jnp.bfloat16)
        turned_minus = (cosine_wide * minus_part - sine_wide * plus_part).astype(jnp.bfloat16)
        split_at = count_of_rows * feature_width
        stacked = jnp.concatenate([turned_plus.reshape(edge_count, split_at), turned_minus.reshape(edge_count, split_at)], axis=0)
        product = jnp.dot(stacked, weight_pair, preferred_element_type=jnp.float32)
        upper_half = product[:edge_count]
        lower_half = product[edge_count:]
        mixed_plus = (upper_half[:, :split_at] - lower_half[:, split_at:]).reshape(edge_count, count_of_rows, feature_width)
        mixed_minus = (upper_half[:, split_at:] + lower_half[:, :split_at]).reshape(edge_count, count_of_rows, feature_width)
        back_plus = neighbour_sum(cosine_wide * mixed_plus - sine_wide * mixed_minus)
        back_minus = neighbour_sum(sine_wide * mixed_plus + cosine_wide * mixed_minus)
        for position_in, degree in enumerate(degrees):
            collected[harmonic_slot(degree, harmonic_order)] = back_plus[:, position_in]
            collected[harmonic_slot(degree, -harmonic_order)] = back_minus[:, position_in]
    zero_block = jnp.zeros((atom_count, feature_width), jnp.float32)
    return jnp.stack([collected.get(slot_number, zero_block) for slot_number in range(25)], axis=1)

def reference(node_irreps, positions, send_list, neighbours, displacements, order_zero, order_one, order_two, reciprocal_triples, reciprocal_filter, cotangent):
    blocks_total = BLOCKS_X * BLOCKS_Y * BLOCKS_Z
    irreps_flat = node_irreps.reshape(blocks_total, ATOMS_DEV, HARMONICS, CHANNEL_COUNT)
    sent_flat = jax.vmap(lambda block_rows, chosen: block_rows[chosen])(irreps_flat, send_list.reshape(blocks_total, GHOSTS))
    displacement_flat = displacements.reshape(blocks_total, 3, ATOMS_DEV * NEIGHBOURS)
    neighbour_flat = neighbours.reshape(blocks_total, ATOMS_DEV, NEIGHBOURS)
    layout = kept_rows(True)

    def one_block(flat_block):
        block_x = flat_block // (BLOCKS_Y * BLOCKS_Z)
        block_y = flat_block // BLOCKS_Z % BLOCKS_Y
        block_z = flat_block % BLOCKS_Z
        pieces = []
        for shift_x in range(3):
            for shift_y in range(3):
                for shift_z in range(3):
                    other_x = (block_x + shift_x - 1) % BLOCKS_X
                    other_y = (block_y + shift_y - 1) % BLOCKS_Y
                    other_z = (block_z + shift_z - 1) % BLOCKS_Z
                    other_block = (other_x * BLOCKS_Y + other_y) * BLOCKS_Z + other_z
                    pieces.append(sent_flat[other_block.astype(jnp.int32)])
        lookup_table = jnp.concatenate([irreps_flat[flat_block]] + pieces, axis=0)
        messages = edge_messages(lookup_table, displacement_flat[flat_block], neighbour_flat[flat_block], order_zero, order_one, order_two, layout)
        return (irreps_flat[flat_block].astype(jnp.float32) + messages).astype(jnp.bfloat16)
    updated = lax.map(one_block, jnp.arange(blocks_total, dtype=jnp.int32)).reshape(node_irreps.shape)
    total_atom_count = ATOMS_DEV * blocks_total
    scale_factor = 1.0 / math.sqrt(total_atom_count * WAVE_VECTORS)
    corner = jnp.stack(jnp.meshgrid(jnp.arange(BLOCKS_X), jnp.arange(BLOCKS_Y), jnp.arange(BLOCKS_Z), indexing='ij'), axis=-1).astype(jnp.float32)
    global_place = positions + cell_length * corner[:, :, :, :, None]
    box = cell_length * jnp.array([BLOCKS_X, BLOCKS_Y, BLOCKS_Z], jnp.float32)
    fractional = global_place / box[:, None]
    fractional = jnp.transpose(fractional, (0, 1, 2, 4, 3)).reshape(total_atom_count, 3)
    wave_float = reciprocal_triples.astype(jnp.float32)
    phase = 2.0 * math.pi * jnp.dot(fractional, wave_float.T, precision=highest)
    cos_table = jnp.cos(phase)
    sin_table = jnp.sin(phase)
    charges = node_irreps[:, :, :, :, 0, :].astype(jnp.float32).reshape(total_atom_count, CHANNEL_COUNT)
    centered = charges - lax.optimization_barrier(jnp.sum(charges, axis=0)) / total_atom_count
    struct_cos = jnp.dot(cos_table.T, centered, precision=highest)
    struct_sin = jnp.dot(sin_table.T, centered, precision=highest)
    long_range = scale_factor * (jnp.dot(cos_table, reciprocal_filter * struct_cos, precision=highest) + jnp.dot(sin_table, reciprocal_filter * struct_sin, precision=highest))
    grad_input = cotangent.reshape(total_atom_count, CHANNEL_COUNT)
    resp_cos = jnp.dot(cos_table.T, grad_input, precision=highest)
    resp_sin = jnp.dot(sin_table.T, grad_input, precision=highest)
    charge_term = scale_factor * (jnp.dot(cos_table, reciprocal_filter * resp_cos, precision=highest) + jnp.dot(sin_table, reciprocal_filter * resp_sin, precision=highest))
    charge_grad = charge_term - lax.optimization_barrier(jnp.sum(charge_term, axis=0)) / total_atom_count
    with_sin = jnp.dot(grad_input, (reciprocal_filter * struct_sin).T, precision=highest) + jnp.dot(centered, (reciprocal_filter * resp_sin).T, precision=highest)
    with_cos = jnp.dot(grad_input, (reciprocal_filter * struct_cos).T, precision=highest) + jnp.dot(centered, (reciprocal_filter * resp_cos).T, precision=highest)
    phase_grad = scale_factor * (cos_table * with_sin - sin_table * with_cos)
    position_grad = 2.0 * math.pi * jnp.dot(phase_grad, wave_float, precision=highest) / box
    position_grad = jnp.transpose(position_grad.reshape(BLOCKS_X, BLOCKS_Y, BLOCKS_Z, ATOMS_DEV, 3), (0, 1, 2, 4, 3))
    shape_out = (BLOCKS_X, BLOCKS_Y, BLOCKS_Z, ATOMS_DEV, CHANNEL_COUNT)
    return (updated, long_range.reshape(shape_out), charge_grad.reshape(shape_out), position_grad)
```

```python
import math

import jax
import jax.numpy as jnp
from jax import lax
from jax.experimental import pallas as pl
from jax.experimental.pallas import tpu as pltpu
from jax.sharding import PartitionSpec as P

MESH = pl.DeviceIdType.MESH
F32 = jnp.float32
BF16 = jnp.bfloat16

cell_length = 6.8
planar_floor = 0.25
radial_width = 64.0
atoms_total = 8192
wave_vectors = 1024
side = 8

GROUP = 16
PEERS = 32
CENTER = 13

half_zero = (0, 2, 6, 12, 20, 3, 7, 13, 21)
half_one = (1, 5, 11, 19, 8, 14, 22, 4, 10, 18)
untouched = (9, 15, 16, 17, 23, 24)


def split(values):
    high = values.astype(BF16)
    return high, (values - high.astype(F32)).astype(BF16)


def dot(a, b, dims=((1,), (0,))):
    return lax.dot_general(a, b, (dims, ((), ())), preferred_element_type=F32)


def dot3(a, b, dims=((1,), (0,))):
    a_high, a_low = split(a)
    b_high, b_low = split(b)
    return dot(a_high, b_high, dims) + (dot(a_high, b_low, dims) + dot(a_low, b_high, dims))


def cos_turns(turns):
    reduced = jnp.abs(turns - jnp.round(turns)) - 0.25
    square = reduced * reduced
    total = jnp.full_like(square, 0.0)
    for power in (13, 11, 9, 7, 5, 3, 1):
        sign = 1.0 if power % 4 == 1 else -1.0
        total = total * square + (-sign * (2.0 * math.pi) ** power / math.factorial(power))
    return total * reduced


def iota(shape, dim):
    return lax.broadcasted_iota(jnp.int32, shape, dim)


def kernel(
    node_ref,
    pos_ref,
    send_ref,
    nb_ref,
    disp_ref,
    w0_hbm,
    w1_hbm,
    w2_hbm,
    trip_ref,
    filt_hbm,
    cot_ref,
    out_ref,
    long_ref,
    charge_ref,
    pgrad_ref,
    table,
    w0,
    w1,
    w2,
    filt,
    atoms,
    trip,
    tiles,
    tiles_in,
    extra_in,
    summed,
    extra,
    part,
    part_in,
    load_sem,
    halo_send,
    halo_z,
    halo_y,
    halo_x,
    send_sem,
    recv_sem,
):
    px, py, pz = lax.axis_index("gx"), lax.axis_index("gy"), lax.axis_index("gz")
    group = (pz // 2) * 4 + (px % 2) * 2 + py % 2
    peer = (px // 2) * 8 + (py // 2) * 2 + pz % 2

    def place(g, r):
        return (
            (r // 8) * 2 + (g // 2) % 2,
            ((r // 2) % 4) * 2 + g % 2,
            (g // 4) * 2 + r % 2,
        )

    def mate(j):
        other = (group + j) % GROUP
        return other, place(other, peer)

    def fellow(j):
        other = (peer + j) % PEERS
        return other, place(group, other)

    around_x = ((px + 1) % side, py, pz), ((px + side - 1) % side, py, pz)
    around_y = (px, (py + 1) % side, pz), (px, (py + side - 1) % side, pz)
    around_z = (px, py, (pz + 1) % side), (px, py, (pz + side - 1) % side)

    def wait_bytes(ref, sem):
        pltpu.make_async_copy(ref, ref, sem).wait()

    barrier = pltpu.get_barrier_semaphore()

    def greet(device):
        pl.semaphore_signal(barrier, inc=1, device_id=device, device_id_type=MESH)

    def greet_mate(j, carry):
        greet(mate(j)[1])
        return carry

    def greet_fellow(j, carry):
        greet(fellow(j)[1])
        return carry

    lax.fori_loop(1, GROUP, greet_mate, 0)
    lax.fori_loop(1, PEERS, greet_fellow, 0)
    for device in around_x + around_y + around_z:
        greet(device)

    loads = [
        pltpu.make_async_copy(
            filt_hbm.at[pl.ds(pl.multiple_of(group * 64, 64), 64), :], filt, load_sem.at[0]
        ),
        pltpu.make_async_copy(w0_hbm, w0, load_sem.at[1]),
        pltpu.make_async_copy(w1_hbm, w1, load_sem.at[2]),
        pltpu.make_async_copy(w2_hbm, w2, load_sem.at[3]),
    ]
    for load in loads:
        load.start()

    atoms[group, 0:16, :] = node_ref[0].astype(F32)
    atoms[group, 16:32, :] = cot_ref[...]
    atoms[group, 32:40, :] = jnp.zeros((8, 128), F32)
    for axis, index in enumerate((px, py, pz)):
        corner = cell_length * index.astype(F32)
        atoms[group, 32 + axis : 33 + axis, 0:16] = (pos_ref[axis] + corner) / (
            cell_length * side
        )

    own_zero = jnp.concatenate(
        [node_ref[s] for s in half_zero] + [jnp.zeros((16, 128), BF16)], axis=1
    )
    own_one = jnp.concatenate([node_ref[s] for s in half_one], axis=1)
    sent = jnp.sum(
        jnp.where(
            iota((16, 8), 0) % 8 == iota((16, 8), 1),
            jnp.broadcast_to(send_ref[...], (16, 8)).astype(F32),
            0.0,
        ),
        axis=1,
        keepdims=True,
    )
    chosen = jnp.where(iota((16, 16), 1).astype(F32) == sent, 1.0, 0.0).astype(BF16)
    upper = iota((16, 1280), 0) < 8
    table[CENTER] = jnp.where(upper, dot(chosen, own_zero), dot(chosen, own_one)).astype(BF16)

    pl.semaphore_wait(barrier, GROUP - 1 + PEERS - 1 + 6)

    def send_atoms(j, carry):
        pltpu.make_async_remote_copy(
            src_ref=atoms.at[group],
            dst_ref=atoms.at[group],
            send_sem=send_sem.at[0],
            recv_sem=recv_sem.at[0],
            device_id=mate(j)[1],
            device_id_type=MESH,
        ).start()
        return carry

    lax.fori_loop(1, GROUP, send_atoms, 0)

    def pass_on(first, count, to, device, sem):
        pltpu.make_async_remote_copy(
            src_ref=table.at[pl.ds(first, count)],
            dst_ref=table.at[pl.ds(to, count)],
            send_sem=halo_send,
            recv_sem=sem,
            device_id=device,
            device_id_type=MESH,
        ).start()

    def along_z(first, count):
        pass_on(first, count, first - 1, around_z[0], halo_z.at[0])
        pass_on(first, count, first + 1, around_z[1], halo_z.at[1])

    def along_y(first, count):
        pass_on(first, count, first - 3, around_y[0], halo_y.at[0])
        pass_on(first, count, first + 3, around_y[1], halo_y.at[1])

    def along_x(first, count):
        pass_on(first, count, first - 9, around_x[0], halo_x.at[0])
        pass_on(first, count, first + 9, around_x[1], halo_x.at[1])

    along_z(CENTER, 1)
    along_y(CENTER, 1)
    along_x(CENTER, 1)

    own_zero_wide, own_one_wide = own_zero.astype(F32), own_one.astype(F32)
    for part_of in range(2):
        rows = slice(8 * part_of, 8 * part_of + 8)
        table[27 + part_of] = jnp.concatenate(
            [own_zero_wide[rows], own_one_wide[rows]], axis=0
        ).astype(BF16)
    for spare in range(29, 32):
        table[spare] = jnp.zeros((16, 1280), BF16)

    block = trip_ref[:, pl.ds(pl.multiple_of((group // 2) * 128, 128), 128)].astype(F32)
    trip[...] = jnp.zeros((8, 128), F32)
    trip[0:3, :] = block
    block = trip[...]
    triples = jnp.where(
        iota((8, 128), 1) // 64 == group % 2, block, pltpu.roll(block, 64, axis=1)
    )
    triples_down = triples.T

    d0, d1, d2 = disp_ref[0], disp_ref[1], disp_ref[2]
    radial = jnp.exp(-(d0 * d0 + d1 * d1 + d2 * d2) / radial_width) / math.sqrt(32)
    planar = jnp.sqrt(d0 * d0 + d1 * d1 + planar_floor)
    cos_one, sin_one = d0 / planar, d1 / planar
    cos_two, sin_two = cos_one * cos_one - sin_one * sin_one, 2.0 * cos_one * sin_one
    edge_weights = (
        radial,
        radial * (cos_one * cos_one + sin_one * sin_one),
        radial * (cos_two * cos_two + sin_two * sin_two),
    )
    of_atom = iota((16, 512), 1) // 32 == iota((16, 512), 0)
    repeat = jnp.where(iota((32, 512), 1) % 32 == iota((32, 512), 0), 1.0, 0.0).astype(BF16)
    named = dot(nb_ref[...].astype(F32).astype(BF16), repeat)
    named = jnp.sum(jnp.where(of_atom, named, 0.0), axis=0, keepdims=True)
    row = iota((512, 128), 0)
    place_of, atom_of = row // 16, row % 16
    listed = jnp.where(
        place_of < 27, 16 + 8 * place_of + atom_of, 8 * (place_of - 27) + atom_of
    )
    listed = jnp.where((atom_of < 8) & (place_of < 29), listed, -1).astype(F32)
    hits = jnp.concatenate(
        [
            jnp.where(named[:, 128 * b : 128 * b + 128] == listed, 1.0, 0.0).astype(BF16)
            for b in range(4)
        ],
        axis=1,
    )
    weight_rows = []
    for weight in edge_weights:
        for piece in split(jnp.where(of_atom, jnp.broadcast_to(weight, (16, 512)), 0.0)):
            weight_rows.append(piece)
    gathered = dot(jnp.concatenate(weight_rows, axis=0), hits, ((1,), (1,)))
    by_order = [gathered[32 * m : 32 * m + 16] + gathered[32 * m + 16 : 32 * m + 32] for m in range(3)]
    mixers = []
    for values in (
        by_order[0],
        by_order[1],
        pltpu.roll(by_order[1], 8, axis=1),
        pltpu.roll(by_order[2], 8, axis=1),
    ):
        mixers.extend(split(values))
    mixers = jnp.concatenate(mixers, axis=0)

    wait_bytes(atoms.at[pl.ds(0, GROUP - 1)], recv_sem.at[0])
    charges = atoms[:, 0:16, :].reshape(256, 128)
    grad_input = atoms[:, 16:32, :].reshape(256, 128)
    places = []
    for low in (0, 8):
        total = atoms[low, 32:40, :]
        for step in range(1, 8):
            total = total + pltpu.roll(atoms[low + step, 32:40, :], 16 * step, axis=1)
        places.append(total)
    places = jnp.concatenate(places, axis=1)
    turns = (
        triples_down[:, 0:1] * places[0:1, :]
        + triples_down[:, 1:2] * places[1:2, :]
        + triples_down[:, 2:3] * places[2:3, :]
    )
    is_sine = iota((128, 256), 0) >= 64
    waves = cos_turns(turns - jnp.where(is_sine, 0.25, 0.0))
    waves_high, waves_low = split(waves)
    charges_half = charges.astype(BF16)
    grad_high, grad_low = split(grad_input)
    raw = dot(waves_high, charges_half) + dot(waves_low, charges_half)
    response = dot(waves_high, grad_high) + (
        dot(waves_high, grad_low) + dot(waves_low, grad_high)
    )
    waves_across = waves.T
    tiles[0:16] = raw.reshape(16, 8, 128)
    tiles[16:32] = response.reshape(16, 8, 128)
    row8 = iota((8, 128), 0)
    tiles[32] = jnp.where(
        row8 == 0,
        jnp.sum(waves_across, axis=0, keepdims=True),
        jnp.where(row8 == 1, jnp.sum(charges, axis=0, keepdims=True), 0.0),
    )

    def send_tile(j, carry):
        other, device = fellow(j)
        pltpu.make_async_remote_copy(
            src_ref=tiles.at[other],
            dst_ref=tiles_in.at[j - 1],
            send_sem=send_sem.at[1],
            recv_sem=recv_sem.at[1],
            device_id=device,
            device_id_type=MESH,
        ).start()
        return carry

    @pl.when(peer != 0)
    def _():
        pltpu.make_async_remote_copy(
            src_ref=tiles.at[PEERS],
            dst_ref=extra_in.at[peer - 1],
            send_sem=send_sem.at[2],
            recv_sem=recv_sem.at[2],
            device_id=place(group, 0),
            device_id_type=MESH,
        ).start()

    lax.fori_loop(1, PEERS, send_tile, 0)

    wait_bytes(table.at[12], halo_z.at[0])
    wait_bytes(table.at[14], halo_z.at[1])
    for piece in (12, 14):
        along_y(piece, 1)
    for piece in (12, 14):
        along_x(piece, 1)

    wait_bytes(tiles_in, recv_sem.at[1])
    summed[peer] = tiles[peer] + jnp.sum(tiles_in[...], axis=0)

    def send_sum(j, carry):
        pltpu.make_async_remote_copy(
            src_ref=summed.at[peer],
            dst_ref=summed.at[peer],
            send_sem=send_sem.at[3],
            recv_sem=recv_sem.at[3],
            device_id=fellow(j)[1],
            device_id_type=MESH,
        ).start()
        return carry

    lax.fori_loop(1, PEERS, send_sum, 0)

    @pl.when(peer == 0)
    def _():
        wait_bytes(extra_in, recv_sem.at[2])
        extra[...] = tiles[PEERS] + jnp.sum(extra_in[...], axis=0)

        def send_extra(j, carry):
            pltpu.make_async_remote_copy(
                src_ref=extra,
                dst_ref=extra,
                send_sem=send_sem.at[4],
                recv_sem=recv_sem.at[4],
                device_id=fellow(j)[1],
                device_id_type=MESH,
            ).start()
            return carry

        lax.fori_loop(1, PEERS, send_extra, 0)

    wait_bytes(table.at[pl.ds(9, 3)], halo_y.at[0])
    along_x(9, 3)
    wait_bytes(table.at[pl.ds(15, 3)], halo_y.at[1])
    along_x(15, 3)

    scale = 1.0 / math.sqrt(atoms_total * wave_vectors)
    loads[0].wait()
    wait_bytes(summed.at[pl.ds(0, PEERS - 1)], recv_sem.at[3])

    @pl.when(peer != 0)
    def _():
        wait_bytes(extra, recv_sem.at[4])

    sums = extra[...]
    mean_charge = sums[1:2, :] / atoms_total
    plane_down = sums.T[:, 0:1]
    factor = filt[...] * scale
    factor = jnp.concatenate([factor, factor], axis=0)
    filtered = factor * (summed[0:16].reshape(128, 128) - plane_down * mean_charge)
    filtered_response = factor * summed[16:32].reshape(128, 128)
    long_part = dot3(waves_across, filtered)
    charge_part = dot3(waves_across - sums[0:1, :] / atoms_total, filtered_response)

    def swapped(values):
        return jnp.concatenate([values[64:], values[:64]], axis=0)

    both = jnp.concatenate([swapped(filtered), swapped(filtered_response)], axis=1)
    sides = jnp.concatenate([grad_input, charges - mean_charge], axis=1)
    phase_grad = waves * dot3(both, sides, ((1,), (1,)))
    signed = jnp.where(iota((8, 128), 1) < 64, triples, -triples).astype(BF16)
    phase_high, phase_low = split(phase_grad)
    pgrad = (dot(signed, phase_high) + dot(signed, phase_low)) * (
        2.0 * math.pi / (cell_length * side)
    )
    part[:, 0:16, :] = long_part.reshape(GROUP, 16, 128)
    part[:, 16:32, :] = charge_part.reshape(GROUP, 16, 128)
    for device in range(GROUP):
        low = 128 * (device // 8)
        values = pgrad[:, low : low + 128]
        if device % 8:
            values = pltpu.roll(values, 128 - 16 * (device % 8), axis=1)
        part[device, 32:40, :] = values

    def send_part(j, carry):
        other, device = mate(j)
        pltpu.make_async_remote_copy(
            src_ref=part.at[other],
            dst_ref=part_in.at[j - 1],
            send_sem=send_sem.at[5],
            recv_sem=recv_sem.at[5],
            device_id=device,
            device_id_type=MESH,
        ).start()
        return carry

    lax.fori_loop(1, GROUP, send_part, 0)

    wait_bytes(table.at[pl.ds(0, 9)], halo_x.at[0])
    wait_bytes(table.at[pl.ds(18, 9)], halo_x.at[1])
    collected = dot(mixers, table[...].reshape(512, 1280))

    def pair(first, lanes):
        return collected[first : first + 16, lanes] + collected[first + 16 : first + 32, lanes]

    loads[1].wait()
    mixed = dot(jnp.concatenate(split(pair(0, slice(0, 640))), axis=0), w0[...])
    mixed = mixed[0:16] + mixed[16:32]
    messages = {l * l + l: mixed[:, 128 * l : 128 * l + 128] for l in range(5)}
    for order, plus, minus, load, weights in (
        (1, pair(32, slice(640, 1152)), pair(64, slice(0, 512)), loads[2], w1),
        (2, pair(96, slice(512, 896)), pair(96, slice(896, 1280)), loads[3], w2),
    ):
        load.wait()
        wide = (5 - order) * 128
        product = dot(jnp.concatenate(split(plus) + split(minus), axis=0), weights[...])
        from_plus = product[0:16] + product[16:32]
        from_minus = product[32:48] + product[48:64]
        mixed_plus = from_plus[:, :wide] - from_minus[:, wide:]
        mixed_minus = from_minus[:, :wide] + from_plus[:, wide:]
        for at, degree in enumerate(range(order, 5)):
            center = degree * degree + degree
            messages[center + order] = mixed_plus[:, 128 * at : 128 * at + 128]
            messages[center - order] = mixed_minus[:, 128 * at : 128 * at + 128]
    for slot, message in messages.items():
        out_ref[slot] = (node_ref[slot].astype(F32) + message).astype(BF16)
    for slot in untouched:
        out_ref[slot] = node_ref[slot]

    wait_bytes(part_in, recv_sem.at[5])
    result = part[group] + jnp.sum(part_in[...], axis=0)
    long_ref[...] = result[0:16]
    charge_ref[...] = result[16:32]
    for axis in range(3):
        pgrad_ref[axis] = result[32 + axis : 33 + axis, 0:16]

    wait_bytes(table.at[pl.ds(0, 26)], halo_send)
    wait_bytes(part_in, send_sem.at[0])
    wait_bytes(tiles_in, send_sem.at[1])

    @pl.when(peer != 0)
    def _():
        wait_bytes(extra, send_sem.at[2])

    wait_bytes(tiles_in, send_sem.at[3])

    @pl.when(peer == 0)
    def _():
        wait_bytes(tiles_in, send_sem.at[4])

    wait_bytes(part_in, send_sem.at[5])


def local(
    node_irreps,
    positions,
    send_list,
    neighbours,
    displacements,
    order_zero,
    order_one,
    order_two,
    reciprocal_triples,
    reciprocal_filter,
    cotangent,
):
    vmem = pl.BlockSpec(memory_space=pltpu.VMEM)
    far = pl.BlockSpec(memory_space=pl.ANY)
    updated, long_range, charge_grad, position_grad = pl.pallas_call(
        kernel,
        out_shape=(
            jax.ShapeDtypeStruct((25, 16, 128), BF16),
            jax.ShapeDtypeStruct((16, 128), F32),
            jax.ShapeDtypeStruct((16, 128), F32),
            jax.ShapeDtypeStruct((3, 1, 16), F32),
        ),
        in_specs=[vmem, vmem, vmem, vmem, vmem, far, far, far, vmem, far, vmem],
        out_specs=(vmem, vmem, vmem, vmem),
        scratch_shapes=[
            pltpu.VMEM((32, 16, 1280), BF16),
            pltpu.VMEM((640, 640), BF16),
            pltpu.VMEM((512, 1024), BF16),
            pltpu.VMEM((384, 768), BF16),
            pltpu.VMEM((64, 128), F32),
            pltpu.VMEM((GROUP, 40, 128), F32),
            pltpu.VMEM((8, 128), F32),
            pltpu.VMEM((PEERS + 1, 8, 128), F32),
            pltpu.VMEM((PEERS - 1, 8, 128), F32),
            pltpu.VMEM((PEERS - 1, 8, 128), F32),
            pltpu.VMEM((PEERS, 8, 128), F32),
            pltpu.VMEM((8, 128), F32),
            pltpu.VMEM((GROUP, 40, 128), F32),
            pltpu.VMEM((GROUP - 1, 40, 128), F32),
            pltpu.SemaphoreType.DMA((4,)),
            pltpu.SemaphoreType.DMA,
            pltpu.SemaphoreType.DMA((2,)),
            pltpu.SemaphoreType.DMA((2,)),
            pltpu.SemaphoreType.DMA((2,)),
            pltpu.SemaphoreType.DMA((6,)),
            pltpu.SemaphoreType.DMA((6,)),
        ],
        compiler_params=pltpu.CompilerParams(
            collective_id=0, has_side_effects=True, vmem_limit_bytes=40 * 1024 * 1024
        ),
    )(
        jnp.transpose(node_irreps[0, 0, 0], (1, 0, 2)),
        positions.reshape(3, 1, 16),
        send_list.reshape(1, 8),
        neighbours.reshape(16, 32),
        displacements.reshape(3, 1, 512),
        order_zero,
        order_one,
        order_two,
        reciprocal_triples.T,
        reciprocal_filter,
        cotangent.reshape(16, 128),
    )
    return (
        jnp.transpose(updated, (1, 0, 2))[None, None, None],
        long_range[None, None, None],
        charge_grad[None, None, None],
        position_grad.reshape(1, 1, 1, 3, 16),
    )


def solution(mesh):
    by_block = ("gx", "gy", "gz")
    return jax.shard_map(
        local,
        mesh=mesh,
        in_specs=(
            P(*by_block, None, None, None),
            P(*by_block, None, None),
            P(*by_block, None),
            P(*by_block, None, None),
            P(*by_block, None, None),
            P(),
            P(),
            P(),
            P(),
            P(),
            P(*by_block, None, None),
        ),
        out_specs=(
            P(*by_block, None, None, None),
            P(*by_block, None, None),
            P(*by_block, None, None),
            P(*by_block, None, None),
        ),
        check_vma=False,
    )
```

```python
import math

import jax
import jax.numpy as jnp
from jax import lax
from jax.experimental import pallas as pl
from jax.experimental.pallas import tpu as pltpu
from jax.sharding import PartitionSpec as P

MESH = pl.DeviceIdType.MESH
F32 = jnp.float32
BF16 = jnp.bfloat16

cell_length = 6.8
planar_floor = 0.25
radial_width = 64.0
atoms_total = 8192
wave_vectors = 1024
side = 8

GROUP = 16
PEERS = 32
CENTER = 13
ROWS = 10

half_zero = (0, 2, 6, 12, 20, 3, 7, 13, 21)
half_one = (1, 5, 11, 19, 8, 14, 22, 4, 10, 18)
untouched = (9, 15, 16, 17, 23, 24)


x_hops, y_hops = (0, 1, 2, 1), (0, 4, 1, 3, 2, 2, 2, 2)
mates = sorted(range(1, GROUP), key=lambda bits: -(x_hops[bits >> 2] + (bits >> 1) % 2))
fellows = sorted(
    range(1, PEERS), key=lambda bits: -(y_hops[bits % 8] + (0, 2, 4, 2)[bits >> 3])
)
along_ring = [bits for bits in fellows if bits < 8]
across_rings = [bits for bits in fellows if bits % 8 == 0]


def split(values):
    high = values.astype(BF16)
    return high, (values - high.astype(F32)).astype(BF16)


def dot(a, b, dims=((1,), (0,))):
    return lax.dot_general(a, b, (dims, ((), ())), preferred_element_type=F32)


def dot3(a, b, dims=((1,), (0,))):
    a_high, a_low = split(a)
    b_high, b_low = split(b)
    return dot(a_high, b_high, dims) + (dot(a_high, b_low, dims) + dot(a_low, b_high, dims))


def cos_turns(turns):
    reduced = jnp.abs(turns - jnp.round(turns)) - 0.25
    square = reduced * reduced
    total = jnp.full_like(square, 0.0)
    for power in (13, 11, 9, 7, 5, 3, 1):
        sign = 1.0 if power % 4 == 1 else -1.0
        total = total * square + (-sign * (2.0 * math.pi) ** power / math.factorial(power))
    return total * reduced


def iota(shape, dim):
    return lax.broadcasted_iota(jnp.int32, shape, dim)


def kernel(
    node_hbm,
    pos_hbm,
    send_hbm,
    nb_hbm,
    disp_hbm,
    w0_hbm,
    w1_hbm,
    w2_hbm,
    trip_hbm,
    filt_hbm,
    cot_hbm,
    out_hbm,
    long_hbm,
    charge_hbm,
    pgrad_hbm,
    first_ref,
    node_ref,
    pos_ref,
    send_ref,
    nb_ref,
    disp_ref,
    w0,
    w1,
    w2,
    trip_ref,
    filt,
    cot_ref,
    out_ref,
    result_ref,
    pgrad_ref,
    table,
    atoms,
    trip,
    tiles,
    tiles_in,
    summed,
    part,
    part_in,
    load_sem,
    store_sem,
    halo_send,
    halo_z,
    halo_y,
    halo_x,
    send_sem,
    recv_sem,
    ring_sem,
):
    px, py, pz = lax.axis_index("gx"), lax.axis_index("gy"), lax.axis_index("gz")
    group = (pz // 2) * 4 + (px % 2) * 2 + py % 2
    peer = (px // 2) * 8 + (py // 2) * 2 + pz % 2

    def turns_of(p):
        return 1 - 2 * (p % 2), 2 - 4 * ((p // 2) % 2), 4 - 8 * (p // 4)

    x_turns, y_turns, z_turns = turns_of(px), turns_of(py), turns_of(pz)
    group_turns = (y_turns[0], 2 * x_turns[0], 2 * z_turns[1], 2 * z_turns[2])
    peer_turns = (z_turns[0], y_turns[1], y_turns[2], 4 * x_turns[1], 4 * x_turns[2])

    def turned(start, bits, steps):
        for at, step in enumerate(steps):
            if (bits >> at) % 2:
                start = start + step
        return start

    def mate(bits):
        return turned(group, bits, group_turns), (
            turned(px, bits >> 1 & 1, x_turns),
            turned(py, bits & 1, y_turns),
            turned(pz, (bits >> 2) << 1, z_turns),
        )

    def fellow(bits):
        return turned(peer, bits, peer_turns), (
            turned(px, (bits >> 3) << 1, x_turns),
            turned(py, (bits >> 1 & 3) << 1, y_turns),
            turned(pz, bits & 1, z_turns),
        )

    around_x = ((px + 1) % side, py, pz), ((px + side - 1) % side, py, pz)
    around_y = (px, (py + 1) % side, pz), (px, (py + side - 1) % side, pz)
    around_z = (px, py, (pz + 1) % side), (px, py, (pz + side - 1) % side)

    def wait_bytes(ref, sem):
        pltpu.make_async_copy(ref, ref, sem).wait()

    slab = pl.multiple_of(group * 64, 64)
    loads = [
        pltpu.make_async_copy(source, target, load_sem.at[at])
        for at, (source, target) in enumerate(
            (
                (node_hbm.at[0], first_ref),
                (cot_hbm, cot_ref),
                (pos_hbm, pos_ref),
                (node_hbm, node_ref),
                (send_hbm, send_ref),
                (trip_hbm, trip_ref),
                (disp_hbm, disp_ref),
                (nb_hbm, nb_ref),
                (filt_hbm.at[pl.ds(slab, 64), :], filt),
                (w0_hbm, w0),
                (w1_hbm, w1),
                (w2_hbm, w2),
            )
        )
    ]
    for load in loads:
        load.start()

    barrier = pltpu.get_barrier_semaphore()

    def greet(device):
        pl.semaphore_signal(barrier, inc=1, device_id=device, device_id_type=MESH)

    for bits in along_ring + across_rings:
        greet(fellow(bits)[1])
    for device in around_z + around_y + around_x:
        greet(device)
    for bits in mates:
        greet(mate(bits)[1])

    for load in loads[:3]:
        load.wait()
    atoms[group, 0:16, :] = first_ref[...].astype(F32)
    atoms[group, 16:32, :] = cot_ref[...]
    atoms[group, 32:40, :] = jnp.zeros((8, 128), F32)
    for axis, index in enumerate((px, py, pz)):
        corner = cell_length * index.astype(F32)
        atoms[group, 32 + axis : 33 + axis, 0:16] = (pos_ref[axis] + corner) / (
            cell_length * side
        )

    pl.semaphore_wait(barrier, len(mates) + len(along_ring) + len(across_rings) + 6)

    for bits in mates:
        pltpu.make_async_remote_copy(
            src_ref=atoms.at[group],
            dst_ref=atoms.at[group],
            send_sem=send_sem.at[0],
            recv_sem=recv_sem.at[0],
            device_id=mate(bits)[1],
            device_id_type=MESH,
        ).start()

    for bits in across_rings:
        pl.semaphore_signal(
            ring_sem, inc=1, device_id=fellow(bits)[1], device_id_type=MESH
        )

    for load in loads[3:5]:
        load.wait()
    own_zero = jnp.concatenate(
        [node_ref[s] for s in half_zero] + [jnp.zeros((16, 128), BF16)], axis=1
    )
    own_one = jnp.concatenate([node_ref[s] for s in half_one], axis=1)
    sent = jnp.sum(
        jnp.where(
            iota((16, 8), 0) % 8 == iota((16, 8), 1),
            jnp.broadcast_to(send_ref[...], (16, 8)).astype(F32),
            0.0,
        ),
        axis=1,
        keepdims=True,
    )
    chosen = jnp.where(iota((16, 16), 1).astype(F32) == sent, 1.0, 0.0).astype(BF16)
    upper = iota((16, 1280), 0) < 8
    table[CENTER] = jnp.where(upper, dot(chosen, own_zero), dot(chosen, own_one)).astype(BF16)

    def pass_on(first, count, to, device, sem):
        pltpu.make_async_remote_copy(
            src_ref=table.at[pl.ds(first, count)],
            dst_ref=table.at[pl.ds(to, count)],
            send_sem=halo_send,
            recv_sem=sem,
            device_id=device,
            device_id_type=MESH,
        ).start()

    def along_z(first, count):
        pass_on(first, count, first - 1, around_z[0], halo_z.at[0])
        pass_on(first, count, first + 1, around_z[1], halo_z.at[1])

    def along_y(first, count):
        pass_on(first, count, first - 3, around_y[0], halo_y.at[0])
        pass_on(first, count, first + 3, around_y[1], halo_y.at[1])

    def along_x(first, count):
        pass_on(first, count, first - 9, around_x[0], halo_x.at[0])
        pass_on(first, count, first + 9, around_x[1], halo_x.at[1])

    along_z(CENTER, 1)
    along_y(CENTER, 1)
    along_x(CENTER, 1)

    own_zero_wide, own_one_wide = own_zero.astype(F32), own_one.astype(F32)
    for part_of in range(2):
        rows = slice(8 * part_of, 8 * part_of + 8)
        table[27 + part_of] = jnp.concatenate(
            [own_zero_wide[rows], own_one_wide[rows]], axis=0
        ).astype(BF16)
    for spare in range(29, 32):
        table[spare] = jnp.zeros((16, 1280), BF16)

    for load in loads[5:8]:
        load.wait()
    block = trip_ref[:, pl.ds(pl.multiple_of((group // 2) * 128, 128), 128)].astype(F32)
    trip[...] = jnp.zeros((8, 128), F32)
    trip[0:3, :] = block
    block = trip[...]
    triples = jnp.where(
        iota((8, 128), 1) // 64 == group % 2, block, pltpu.roll(block, 64, axis=1)
    )
    triples_down = triples.T

    d0, d1, d2 = disp_ref[0], disp_ref[1], disp_ref[2]
    radial = jnp.exp(-(d0 * d0 + d1 * d1 + d2 * d2) / radial_width) / math.sqrt(32)
    planar = jnp.sqrt(d0 * d0 + d1 * d1 + planar_floor)
    cos_one, sin_one = d0 / planar, d1 / planar
    cos_two, sin_two = cos_one * cos_one - sin_one * sin_one, 2.0 * cos_one * sin_one
    edge_weights = (
        radial,
        radial * (cos_one * cos_one + sin_one * sin_one),
        radial * (cos_two * cos_two + sin_two * sin_two),
    )
    of_atom = iota((16, 512), 1) // 32 == iota((16, 512), 0)
    repeat = jnp.where(iota((32, 512), 1) % 32 == iota((32, 512), 0), 1.0, 0.0).astype(BF16)
    named = dot(nb_ref[...].astype(F32).astype(BF16), repeat)
    named = jnp.sum(jnp.where(of_atom, named, 0.0), axis=0, keepdims=True)
    row = iota((512, 128), 0)
    place_of, atom_of = row // 16, row % 16
    listed = jnp.where(
        place_of < 27, 16 + 8 * place_of + atom_of, 8 * (place_of - 27) + atom_of
    )
    listed = jnp.where((atom_of < 8) & (place_of < 29), listed, -1).astype(F32)
    hits = jnp.concatenate(
        [
            jnp.where(named[:, 128 * b : 128 * b + 128] == listed, 1.0, 0.0).astype(BF16)
            for b in range(4)
        ],
        axis=1,
    )
    weight_rows = []
    for weight in edge_weights:
        for piece in split(jnp.where(of_atom, jnp.broadcast_to(weight, (16, 512)), 0.0)):
            weight_rows.append(piece)
    gathered = dot(jnp.concatenate(weight_rows, axis=0), hits, ((1,), (1,)))
    by_order = [gathered[32 * m : 32 * m + 16] + gathered[32 * m + 16 : 32 * m + 32] for m in range(3)]
    mixers = []
    for values in (
        by_order[0],
        by_order[1],
        pltpu.roll(by_order[1], 8, axis=1),
        pltpu.roll(by_order[2], 8, axis=1),
    ):
        mixers.extend(split(values))
    mixers = jnp.concatenate(mixers, axis=0)

    wait_bytes(atoms.at[pl.ds(0, GROUP - 1)], recv_sem.at[0])
    charges = atoms[:, 0:16, :].reshape(256, 128)
    grad_input = atoms[:, 16:32, :].reshape(256, 128)
    places = []
    for low in (0, 8):
        total = atoms[low, 32:40, :]
        for step in range(1, 8):
            total = total + pltpu.roll(atoms[low + step, 32:40, :], 16 * step, axis=1)
        places.append(total)
    places = jnp.concatenate(places, axis=1)
    turns = (
        triples_down[:, 0:1] * places[0:1, :]
        + triples_down[:, 1:2] * places[1:2, :]
        + triples_down[:, 2:3] * places[2:3, :]
    )
    is_sine = iota((128, 256), 0) >= 64
    waves = cos_turns(turns - jnp.where(is_sine, 0.25, 0.0))
    waves_high, waves_low = split(waves)
    charges_half = charges.astype(BF16)
    grad_high, grad_low = split(grad_input)
    raw = dot(waves_high, charges_half) + dot(waves_low, charges_half)
    response = dot(waves_high, grad_high) + (
        dot(waves_high, grad_low) + dot(waves_low, grad_high)
    )
    waves_across = waves.T
    tiles[0:16, 0:8, :] = raw.reshape(16, 8, 128)
    tiles[16:32, 0:8, :] = response.reshape(16, 8, 128)
    plane = jnp.sum(waves_across, axis=0, keepdims=True)
    total_charge = jnp.sum(charges, axis=0, keepdims=True)
    extra = jnp.concatenate([plane, total_charge, jnp.zeros((6, 128), F32)], axis=0)
    tiles[:, 8:16, :] = jnp.broadcast_to(extra, (PEERS, 8, 128))

    pl.semaphore_wait(ring_sem, len(across_rings))

    for bits in fellows:
        other, device = fellow(bits)
        pltpu.make_async_remote_copy(
            src_ref=tiles.at[other, pl.ds(0, ROWS)],
            dst_ref=tiles_in.at[bits - 1, pl.ds(0, ROWS)],
            send_sem=send_sem.at[1],
            recv_sem=recv_sem.at[1],
            device_id=device,
            device_id_type=MESH,
        ).start()

    wait_bytes(table.at[12], halo_z.at[0])
    wait_bytes(table.at[14], halo_z.at[1])
    for piece in (12, 14):
        along_y(piece, 1)
    for piece in (12, 14):
        along_x(piece, 1)

    wait_bytes(table.at[pl.ds(9, 3)], halo_y.at[0])
    along_x(9, 3)
    wait_bytes(table.at[pl.ds(15, 3)], halo_y.at[1])
    along_x(15, 3)

    all_tiles = tiles_in.at[:, pl.ds(0, ROWS), :]
    wait_bytes(all_tiles, recv_sem.at[1])
    whole = tiles[peer, 0:ROWS, :] + jnp.sum(tiles_in[:, 0:ROWS, :], axis=0)
    summed[peer] = whole[0:8]
    plane, total_charge = whole[8:9], whole[9:10]
    for bits in fellows:
        pltpu.make_async_remote_copy(
            src_ref=summed.at[peer],
            dst_ref=summed.at[peer],
            send_sem=send_sem.at[2],
            recv_sem=recv_sem.at[2],
            device_id=fellow(bits)[1],
            device_id_type=MESH,
        ).start()

    wait_bytes(table.at[pl.ds(0, 9)], halo_x.at[0])
    wait_bytes(table.at[pl.ds(18, 9)], halo_x.at[1])
    collected = dot(mixers, table[...].reshape(512, 1280))

    def pair(first, lanes):
        return collected[first : first + 16, lanes] + collected[first + 16 : first + 32, lanes]

    loads[9].wait()
    mixed = dot(jnp.concatenate(split(pair(0, slice(0, 640))), axis=0), w0[...])
    mixed = mixed[0:16] + mixed[16:32]
    messages = {l * l + l: mixed[:, 128 * l : 128 * l + 128] for l in range(5)}
    for order, plus, minus, load, weights in (
        (1, pair(32, slice(640, 1152)), pair(64, slice(0, 512)), loads[10], w1),
        (2, pair(96, slice(512, 896)), pair(96, slice(896, 1280)), loads[11], w2),
    ):
        load.wait()
        wide = (5 - order) * 128
        product = dot(jnp.concatenate(split(plus) + split(minus), axis=0), weights[...])
        from_plus = product[0:16] + product[16:32]
        from_minus = product[32:48] + product[48:64]
        mixed_plus = from_plus[:, :wide] - from_minus[:, wide:]
        mixed_minus = from_minus[:, :wide] + from_plus[:, wide:]
        for at, degree in enumerate(range(order, 5)):
            center = degree * degree + degree
            messages[center + order] = mixed_plus[:, 128 * at : 128 * at + 128]
            messages[center - order] = mixed_minus[:, 128 * at : 128 * at + 128]
    for slot, message in messages.items():
        out_ref[slot] = (node_ref[slot].astype(F32) + message).astype(BF16)
    for slot in untouched:
        out_ref[slot] = node_ref[slot]

    scale = 1.0 / math.sqrt(atoms_total * wave_vectors)
    loads[8].wait()
    wait_bytes(summed.at[pl.ds(0, PEERS - 1)], recv_sem.at[2])
    mean_charge = total_charge / atoms_total
    plane_down = jnp.broadcast_to(plane, (8, 128)).T[:, 0:1]
    factor = filt[...] * scale
    factor = jnp.concatenate([factor, factor], axis=0)
    filtered = factor * (summed[0:16].reshape(128, 128) - plane_down * mean_charge)
    filtered_response = factor * summed[16:32].reshape(128, 128)
    long_part = dot3(waves_across, filtered)
    charge_part = dot3(waves_across - plane / atoms_total, filtered_response)

    def swapped(values):
        return jnp.concatenate([values[64:], values[:64]], axis=0)

    both = jnp.concatenate([swapped(filtered), swapped(filtered_response)], axis=1)
    sides = jnp.concatenate([grad_input, charges - mean_charge], axis=1)
    phase_grad = waves * dot3(both, sides, ((1,), (1,)))
    signed = jnp.where(iota((8, 128), 1) < 64, triples, -triples).astype(BF16)
    phase_high, phase_low = split(phase_grad)
    pgrad = (dot(signed, phase_high) + dot(signed, phase_low)) * (
        2.0 * math.pi / (cell_length * side)
    )
    part[:, 0:16, :] = long_part.reshape(GROUP, 16, 128)
    part[:, 16:32, :] = charge_part.reshape(GROUP, 16, 128)
    for device in range(GROUP):
        low = 128 * (device // 8)
        values = pgrad[:, low : low + 128]
        if device % 8:
            values = pltpu.roll(values, 128 - 16 * (device % 8), axis=1)
        part[device, 32:40, :] = values

    for bits in mates:
        other, device = mate(bits)
        pltpu.make_async_remote_copy(
            src_ref=part.at[other],
            dst_ref=part_in.at[bits - 1],
            send_sem=send_sem.at[3],
            recv_sem=recv_sem.at[3],
            device_id=device,
            device_id_type=MESH,
        ).start()

    stores = [
        pltpu.make_async_copy(source, target, store_sem.at[at])
        for at, (source, target) in enumerate(
            (
                (out_ref, out_hbm),
                (result_ref.at[pl.ds(0, 16)], long_hbm),
                (result_ref.at[pl.ds(16, 16)], charge_hbm),
                (pgrad_ref, pgrad_hbm),
            )
        )
    ]
    stores[0].start()

    wait_bytes(part_in, recv_sem.at[3])
    result = part[group] + jnp.sum(part_in[...], axis=0)
    result_ref[...] = result
    for axis in range(3):
        pgrad_ref[axis] = result[32 + axis : 33 + axis, 0:16]
    for store in stores[1:]:
        store.start()

    wait_bytes(table.at[pl.ds(0, 26)], halo_send)
    wait_bytes(part_in, send_sem.at[0])
    wait_bytes(all_tiles, send_sem.at[1])
    wait_bytes(summed.at[pl.ds(0, PEERS - 1)], send_sem.at[2])
    wait_bytes(part_in, send_sem.at[3])
    for store in stores:
        store.wait()


def settle(*refs):
    sources, targets, held, sems = refs[0:4], refs[4:8], refs[8:12], refs[12]
    into = [pltpu.make_async_copy(sources[at], held[at], sems.at[at]) for at in range(4)]
    out = [pltpu.make_async_copy(held[at], targets[at], sems.at[4 + at]) for at in range(4)]
    for copy in into:
        copy.start()
    for arrive, leave in zip(into, out):
        arrive.wait()
        leave.start()
    for copy in out:
        copy.wait()


def local(
    node_irreps,
    positions,
    send_list,
    neighbours,
    displacements,
    order_zero,
    order_one,
    order_two,
    reciprocal_triples,
    reciprocal_filter,
    cotangent,
):
    far = pl.BlockSpec(memory_space=pl.ANY)
    results = (
        jax.ShapeDtypeStruct((25, 16, 128), BF16),
        jax.ShapeDtypeStruct((16, 128), F32),
        jax.ShapeDtypeStruct((16, 128), F32),
        jax.ShapeDtypeStruct((3, 1, 16), F32),
    )
    held = pl.pallas_call(
        kernel,
        out_shape=results,
        in_specs=[far] * 11,
        out_specs=(far,) * 4,
        scratch_shapes=[
            pltpu.VMEM((16, 128), BF16),
            pltpu.VMEM((25, 16, 128), BF16),
            pltpu.VMEM((3, 1, 16), F32),
            pltpu.VMEM((1, 8), jnp.int32),
            pltpu.VMEM((16, 32), jnp.int32),
            pltpu.VMEM((3, 1, 512), F32),
            pltpu.VMEM((640, 640), BF16),
            pltpu.VMEM((512, 1024), BF16),
            pltpu.VMEM((384, 768), BF16),
            pltpu.VMEM((3, 1024), jnp.int32),
            pltpu.VMEM((64, 128), F32),
            pltpu.VMEM((16, 128), F32),
            pltpu.VMEM((25, 16, 128), BF16),
            pltpu.VMEM((40, 128), F32),
            pltpu.VMEM((3, 1, 16), F32),
            pltpu.VMEM((32, 16, 1280), BF16),
            pltpu.VMEM((GROUP, 40, 128), F32),
            pltpu.VMEM((8, 128), F32),
            pltpu.VMEM((PEERS, 16, 128), F32),
            pltpu.VMEM((PEERS - 1, 16, 128), F32),
            pltpu.VMEM((PEERS, 8, 128), F32),
            pltpu.VMEM((GROUP, 40, 128), F32),
            pltpu.VMEM((GROUP - 1, 40, 128), F32),
            pltpu.SemaphoreType.DMA((12,)),
            pltpu.SemaphoreType.DMA((4,)),
            pltpu.SemaphoreType.DMA,
            pltpu.SemaphoreType.DMA((2,)),
            pltpu.SemaphoreType.DMA((2,)),
            pltpu.SemaphoreType.DMA((2,)),
            pltpu.SemaphoreType.DMA((4,)),
            pltpu.SemaphoreType.DMA((4,)),
            pltpu.SemaphoreType.REGULAR,
        ],
        compiler_params=pltpu.CompilerParams(
            collective_id=0, has_side_effects=True, vmem_limit_bytes=60 * 1024 * 1024
        ),
    )(
        jnp.transpose(node_irreps[0, 0, 0], (1, 0, 2)),
        positions.reshape(3, 1, 16),
        send_list.reshape(1, 8),
        neighbours.reshape(16, 32),
        displacements.reshape(3, 1, 512),
        order_zero,
        order_one,
        order_two,
        reciprocal_triples.T,
        reciprocal_filter,
        cotangent.reshape(16, 128),
    )
    updated, long_range, charge_grad, position_grad = pl.pallas_call(
        settle,
        out_shape=results,
        in_specs=[far] * 4,
        out_specs=(far,) * 4,
        scratch_shapes=[pltpu.VMEM(held_one.shape, held_one.dtype) for held_one in results]
        + [pltpu.SemaphoreType.DMA((8,))],
        compiler_params=pltpu.CompilerParams(vmem_limit_bytes=60 * 1024 * 1024),
    )(*held)
    return (
        jnp.transpose(updated, (1, 0, 2))[None, None, None],
        long_range[None, None, None],
        charge_grad[None, None, None],
        position_grad.reshape(1, 1, 1, 3, 16),
    )


def solution(mesh):
    by_block = ("gx", "gy", "gz")
    return jax.shard_map(
        local,
        mesh=mesh,
        in_specs=(
            P(*by_block, None, None, None),
            P(*by_block, None, None),
            P(*by_block, None),
            P(*by_block, None, None),
            P(*by_block, None, None),
            P(),
            P(),
            P(),
            P(),
            P(),
            P(*by_block, None, None),
        ),
        out_specs=(
            P(*by_block, None, None, None),
            P(*by_block, None, None),
            P(*by_block, None, None),
            P(*by_block, None, None),
        ),
        check_vma=False,
    )
```

```python
import math

import jax
import jax.numpy as jnp
from jax import lax
from jax.experimental import pallas as pl
from jax.experimental.pallas import tpu as pltpu
from jax.sharding import PartitionSpec as P

MESH = pl.DeviceIdType.MESH
F32 = jnp.float32
BF16 = jnp.bfloat16

cell_length = 6.8
planar_floor = 0.25
radial_width = 64.0
atoms_total = 8192
wave_vectors = 1024
side = 8

GROUP = 16
PEERS = 32
CENTER = 13
ROWS = 10

half_zero = (0, 2, 6, 12, 20, 3, 7, 13, 21)
half_one = (1, 5, 11, 19, 8, 14, 22, 4, 10, 18)
untouched = (9, 15, 16, 17, 23, 24)


x_hops, y_hops = (0, 1, 2, 1), (0, 4, 1, 3, 2, 2, 2, 2)
mates = sorted(range(1, GROUP), key=lambda bits: -(x_hops[bits >> 2] + (bits >> 1) % 2))
fellows = sorted(
    range(1, PEERS), key=lambda bits: -(y_hops[bits % 8] + (0, 2, 4, 2)[bits >> 3])
)
along_ring = [bits for bits in fellows if bits < 8]
across_rings = [bits for bits in fellows if bits % 8 == 0]


def split(values):
    high = values.astype(BF16)
    return high, (values - high.astype(F32)).astype(BF16)


def dot(a, b, dims=((1,), (0,))):
    return lax.dot_general(a, b, (dims, ((), ())), preferred_element_type=F32)


def dot3(a, b, dims=((1,), (0,))):
    a_high, a_low = split(a)
    b_high, b_low = split(b)
    return dot(a_high, b_high, dims) + (dot(a_high, b_low, dims) + dot(a_low, b_high, dims))


def cos_turns(turns):
    reduced = jnp.abs(turns - jnp.round(turns)) - 0.25
    square = reduced * reduced
    total = jnp.full_like(square, 0.0)
    for power in (13, 11, 9, 7, 5, 3, 1):
        sign = 1.0 if power % 4 == 1 else -1.0
        total = total * square + (-sign * (2.0 * math.pi) ** power / math.factorial(power))
    return total * reduced


def iota(shape, dim):
    return lax.broadcasted_iota(jnp.int32, shape, dim)


def kernel(
    node_hbm,
    pos_hbm,
    send_hbm,
    nb_hbm,
    disp_hbm,
    w0_hbm,
    w1_hbm,
    w2_hbm,
    trip_hbm,
    filt_hbm,
    cot_hbm,
    out_hbm,
    long_hbm,
    charge_hbm,
    pgrad_hbm,
    first_ref,
    node_ref,
    pos_ref,
    send_ref,
    nb_ref,
    disp_ref,
    w0,
    w1,
    w2,
    trip_ref,
    filt,
    cot_ref,
    out_ref,
    result_ref,
    pgrad_ref,
    table,
    atoms,
    trip,
    tiles,
    tiles_in,
    summed,
    part,
    part_in,
    load_sem,
    store_sem,
    halo_send,
    halo_z,
    halo_y,
    halo_x,
    send_sem,
    recv_sem,
    ring_sem,
):
    px, py, pz = lax.axis_index("gx"), lax.axis_index("gy"), lax.axis_index("gz")
    group = (pz // 2) * 4 + (px % 2) * 2 + py % 2
    peer = (px // 2) * 8 + (py // 2) * 2 + pz % 2

    def turns_of(p):
        return 1 - 2 * (p % 2), 2 - 4 * ((p // 2) % 2), 4 - 8 * (p // 4)

    x_turns, y_turns, z_turns = turns_of(px), turns_of(py), turns_of(pz)
    group_turns = (y_turns[0], 2 * x_turns[0], 2 * z_turns[1], 2 * z_turns[2])
    peer_turns = (z_turns[0], y_turns[1], y_turns[2], 4 * x_turns[1], 4 * x_turns[2])

    def turned(start, bits, steps):
        for at, step in enumerate(steps):
            if (bits >> at) % 2:
                start = start + step
        return start

    def mate(bits):
        return turned(group, bits, group_turns), (
            turned(px, bits >> 1 & 1, x_turns),
            turned(py, bits & 1, y_turns),
            turned(pz, (bits >> 2) << 1, z_turns),
        )

    def fellow(bits):
        return turned(peer, bits, peer_turns), (
            turned(px, (bits >> 3) << 1, x_turns),
            turned(py, (bits >> 1 & 3) << 1, y_turns),
            turned(pz, bits & 1, z_turns),
        )

    around_x = ((px + 1) % side, py, pz), ((px + side - 1) % side, py, pz)
    around_y = (px, (py + 1) % side, pz), (px, (py + side - 1) % side, pz)
    around_z = (px, py, (pz + 1) % side), (px, py, (pz + side - 1) % side)

    def wait_bytes(ref, sem):
        pltpu.make_async_copy(ref, ref, sem).wait()

    slab = pl.multiple_of(group * 64, 64)
    loads = [
        pltpu.make_async_copy(source, target, load_sem.at[at])
        for at, (source, target) in enumerate(
            (
                (node_hbm.at[0], first_ref),
                (cot_hbm, cot_ref),
                (pos_hbm, pos_ref),
                (node_hbm, node_ref),
                (send_hbm, send_ref),
                (trip_hbm, trip_ref),
                (disp_hbm, disp_ref),
                (nb_hbm, nb_ref),
                (filt_hbm.at[pl.ds(slab, 64), :], filt),
                (w0_hbm, w0),
                (w1_hbm, w1),
                (w2_hbm, w2),
            )
        )
    ]
    for load in loads:
        load.start()

    barrier = pltpu.get_barrier_semaphore()

    def greet(device):
        pl.semaphore_signal(barrier, inc=1, device_id=device, device_id_type=MESH)

    for bits in along_ring + across_rings:
        greet(fellow(bits)[1])
    for device in around_z + around_y + around_x:
        greet(device)
    for bits in mates:
        greet(mate(bits)[1])

    for load in loads[:3]:
        load.wait()
    atoms[group, 0:16, :] = first_ref[...].astype(F32)
    atoms[group, 16:32, :] = cot_ref[...]
    atoms[group, 32:40, :] = jnp.zeros((8, 128), F32)
    for axis, index in enumerate((px, py, pz)):
        corner = cell_length * index.astype(F32)
        atoms[group, 32 + axis : 33 + axis, 0:16] = (pos_ref[axis] + corner) / (
            cell_length * side
        )

    pl.semaphore_wait(barrier, len(mates) + len(along_ring) + len(across_rings) + 6)

    for bits in mates:
        pltpu.make_async_remote_copy(
            src_ref=atoms.at[group],
            dst_ref=atoms.at[group],
            send_sem=send_sem.at[0],
            recv_sem=recv_sem.at[0],
            device_id=mate(bits)[1],
            device_id_type=MESH,
        ).start()

    for bits in across_rings:
        pl.semaphore_signal(
            ring_sem, inc=1, device_id=fellow(bits)[1], device_id_type=MESH
        )

    for load in loads[3:5]:
        load.wait()
    own_zero = jnp.concatenate(
        [node_ref[s] for s in half_zero] + [jnp.zeros((16, 128), BF16)], axis=1
    )
    own_one = jnp.concatenate([node_ref[s] for s in half_one], axis=1)
    sent = jnp.sum(
        jnp.where(
            iota((16, 8), 0) % 8 == iota((16, 8), 1),
            jnp.broadcast_to(send_ref[...], (16, 8)).astype(F32),
            0.0,
        ),
        axis=1,
        keepdims=True,
    )
    chosen = jnp.where(iota((16, 16), 1).astype(F32) == sent, 1.0, 0.0).astype(BF16)
    upper = iota((16, 1280), 0) < 8
    table[CENTER] = jnp.where(upper, dot(chosen, own_zero), dot(chosen, own_one)).astype(BF16)

    def pass_on(first, count, to, device, sem):
        pltpu.make_async_remote_copy(
            src_ref=table.at[pl.ds(first, count)],
            dst_ref=table.at[pl.ds(to, count)],
            send_sem=halo_send,
            recv_sem=sem,
            device_id=device,
            device_id_type=MESH,
        ).start()

    def along_z(first, count):
        pass_on(first, count, first - 1, around_z[0], halo_z.at[0])
        pass_on(first, count, first + 1, around_z[1], halo_z.at[1])

    def along_y(first, count):
        pass_on(first, count, first - 3, around_y[0], halo_y.at[0])
        pass_on(first, count, first + 3, around_y[1], halo_y.at[1])

    def along_x(first, count):
        pass_on(first, count, first - 9, around_x[0], halo_x.at[0])
        pass_on(first, count, first + 9, around_x[1], halo_x.at[1])

    along_z(CENTER, 1)
    along_y(CENTER, 1)
    along_x(CENTER, 1)

    own_zero_wide, own_one_wide = own_zero.astype(F32), own_one.astype(F32)
    for part_of in range(2):
        rows = slice(8 * part_of, 8 * part_of + 8)
        table[27 + part_of] = jnp.concatenate(
            [own_zero_wide[rows], own_one_wide[rows]], axis=0
        ).astype(BF16)
    for spare in range(29, 32):
        table[spare] = jnp.zeros((16, 1280), BF16)

    for load in loads[5:8]:
        load.wait()
    block = trip_ref[:, pl.ds(pl.multiple_of((group // 2) * 128, 128), 128)].astype(F32)
    trip[...] = jnp.zeros((8, 128), F32)
    trip[0:3, :] = block
    block = trip[...]
    triples = jnp.where(
        iota((8, 128), 1) // 64 == group % 2, block, pltpu.roll(block, 64, axis=1)
    )
    triples_down = triples.T

    d0, d1, d2 = disp_ref[0], disp_ref[1], disp_ref[2]
    radial = jnp.exp(-(d0 * d0 + d1 * d1 + d2 * d2) / radial_width) / math.sqrt(32)
    planar = jnp.sqrt(d0 * d0 + d1 * d1 + planar_floor)
    cos_one, sin_one = d0 / planar, d1 / planar
    cos_two, sin_two = cos_one * cos_one - sin_one * sin_one, 2.0 * cos_one * sin_one
    edge_weights = (
        radial,
        radial * (cos_one * cos_one + sin_one * sin_one),
        radial * (cos_two * cos_two + sin_two * sin_two),
    )
    of_atom = iota((16, 512), 1) // 32 == iota((16, 512), 0)
    repeat = jnp.where(iota((32, 512), 1) % 32 == iota((32, 512), 0), 1.0, 0.0).astype(BF16)
    named = dot(nb_ref[...].astype(F32).astype(BF16), repeat)
    named = jnp.sum(jnp.where(of_atom, named, 0.0), axis=0, keepdims=True)
    row = iota((512, 128), 0)
    place_of, atom_of = row // 16, row % 16
    listed = jnp.where(
        place_of < 27, 16 + 8 * place_of + atom_of, 8 * (place_of - 27) + atom_of
    )
    listed = jnp.where((atom_of < 8) & (place_of < 29), listed, -1).astype(F32)
    hits = jnp.concatenate(
        [
            jnp.where(named[:, 128 * b : 128 * b + 128] == listed, 1.0, 0.0).astype(BF16)
            for b in range(4)
        ],
        axis=1,
    )
    weight_rows = []
    for weight in edge_weights:
        for piece in split(jnp.where(of_atom, jnp.broadcast_to(weight, (16, 512)), 0.0)):
            weight_rows.append(piece)
    gathered = dot(jnp.concatenate(weight_rows, axis=0), hits, ((1,), (1,)))
    by_order = [gathered[32 * m : 32 * m + 16] + gathered[32 * m + 16 : 32 * m + 32] for m in range(3)]
    mixers = []
    for values in (
        by_order[0],
        by_order[1],
        pltpu.roll(by_order[1], 8, axis=1),
        pltpu.roll(by_order[2], 8, axis=1),
    ):
        mixers.extend(split(values))
    mixers = jnp.concatenate(mixers, axis=0)

    wait_bytes(atoms.at[pl.ds(0, GROUP - 1)], recv_sem.at[0])
    charges = atoms[:, 0:16, :].reshape(256, 128)
    grad_input = atoms[:, 16:32, :].reshape(256, 128)
    places = []
    for low in (0, 8):
        total = atoms[low, 32:40, :]
        for step in range(1, 8):
            total = total + pltpu.roll(atoms[low + step, 32:40, :], 16 * step, axis=1)
        places.append(total)
    places = jnp.concatenate(places, axis=1)
    turns = (
        triples_down[:, 0:1] * places[0:1, :]
        + triples_down[:, 1:2] * places[1:2, :]
        + triples_down[:, 2:3] * places[2:3, :]
    )
    is_sine = iota((128, 256), 0) >= 64
    waves = cos_turns(turns - jnp.where(is_sine, 0.25, 0.0))
    waves_high, waves_low = split(waves)
    charges_half = charges.astype(BF16)
    grad_high, grad_low = split(grad_input)
    raw = dot(waves_high, charges_half) + dot(waves_low, charges_half)
    response = dot(waves_high, grad_high) + (
        dot(waves_high, grad_low) + dot(waves_low, grad_high)
    )
    waves_across = waves.T
    tiles[0:16, 0:8, :] = raw.reshape(16, 8, 128)
    tiles[16:32, 0:8, :] = response.reshape(16, 8, 128)
    plane = jnp.sum(waves_across, axis=0, keepdims=True)
    total_charge = jnp.sum(charges, axis=0, keepdims=True)
    extra = jnp.concatenate([plane, total_charge, jnp.zeros((6, 128), F32)], axis=0)
    tiles[:, 8:16, :] = jnp.broadcast_to(extra, (PEERS, 8, 128))

    pl.semaphore_wait(ring_sem, len(across_rings))

    for bits in fellows:
        other, device = fellow(bits)
        pltpu.make_async_remote_copy(
            src_ref=tiles.at[other, pl.ds(0, ROWS)],
            dst_ref=tiles_in.at[bits - 1, pl.ds(0, ROWS)],
            send_sem=send_sem.at[1],
            recv_sem=recv_sem.at[1],
            device_id=device,
            device_id_type=MESH,
        ).start()

    wait_bytes(table.at[12], halo_z.at[0])
    wait_bytes(table.at[14], halo_z.at[1])
    for piece in (12, 14):
        along_y(piece, 1)
    for piece in (12, 14):
        along_x(piece, 1)

    all_tiles = tiles_in.at[:, pl.ds(0, ROWS), :]
    wait_bytes(all_tiles, recv_sem.at[1])
    whole = tiles[peer, 0:ROWS, :] + jnp.sum(tiles_in[:, 0:ROWS, :], axis=0)
    summed[peer] = whole[0:8]
    plane, total_charge = whole[8:9], whole[9:10]
    for bits in fellows:
        pltpu.make_async_remote_copy(
            src_ref=summed.at[peer],
            dst_ref=summed.at[peer],
            send_sem=send_sem.at[2],
            recv_sem=recv_sem.at[2],
            device_id=fellow(bits)[1],
            device_id_type=MESH,
        ).start()

    wait_bytes(table.at[pl.ds(9, 3)], halo_y.at[0])
    along_x(9, 3)
    wait_bytes(table.at[pl.ds(15, 3)], halo_y.at[1])
    along_x(15, 3)

    scale = 1.0 / math.sqrt(atoms_total * wave_vectors)
    loads[8].wait()
    wait_bytes(summed.at[pl.ds(0, PEERS - 1)], recv_sem.at[2])
    mean_charge = total_charge / atoms_total
    plane_down = jnp.broadcast_to(plane, (8, 128)).T[:, 0:1]
    factor = filt[...] * scale
    factor = jnp.concatenate([factor, factor], axis=0)
    filtered = factor * (summed[0:16].reshape(128, 128) - plane_down * mean_charge)
    filtered_response = factor * summed[16:32].reshape(128, 128)
    long_part = dot3(waves_across, filtered)
    charge_part = dot3(waves_across - plane / atoms_total, filtered_response)

    def swapped(values):
        return jnp.concatenate([values[64:], values[:64]], axis=0)

    both = jnp.concatenate([swapped(filtered), swapped(filtered_response)], axis=1)
    sides = jnp.concatenate([grad_input, charges - mean_charge], axis=1)
    phase_grad = waves * dot3(both, sides, ((1,), (1,)))
    signed = jnp.where(iota((8, 128), 1) < 64, triples, -triples).astype(BF16)
    phase_high, phase_low = split(phase_grad)
    pgrad = (dot(signed, phase_high) + dot(signed, phase_low)) * (
        2.0 * math.pi / (cell_length * side)
    )
    part[:, 0:16, :] = long_part.reshape(GROUP, 16, 128)
    part[:, 16:32, :] = charge_part.reshape(GROUP, 16, 128)
    for device in range(GROUP):
        low = 128 * (device // 8)
        values = pgrad[:, low : low + 128]
        if device % 8:
            values = pltpu.roll(values, 128 - 16 * (device % 8), axis=1)
        part[device, 32:40, :] = values

    for bits in mates:
        other, device = mate(bits)
        pltpu.make_async_remote_copy(
            src_ref=part.at[other],
            dst_ref=part_in.at[bits - 1],
            send_sem=send_sem.at[3],
            recv_sem=recv_sem.at[3],
            device_id=device,
            device_id_type=MESH,
        ).start()

    wait_bytes(table.at[pl.ds(0, 9)], halo_x.at[0])
    wait_bytes(table.at[pl.ds(18, 9)], halo_x.at[1])
    collected = dot(mixers, table[...].reshape(512, 1280))

    def pair(first, lanes):
        return collected[first : first + 16, lanes] + collected[first + 16 : first + 32, lanes]

    loads[9].wait()
    mixed = dot(jnp.concatenate(split(pair(0, slice(0, 640))), axis=0), w0[...])
    mixed = mixed[0:16] + mixed[16:32]
    messages = {l * l + l: mixed[:, 128 * l : 128 * l + 128] for l in range(5)}
    for order, plus, minus, load, weights in (
        (1, pair(32, slice(640, 1152)), pair(64, slice(0, 512)), loads[10], w1),
        (2, pair(96, slice(512, 896)), pair(96, slice(896, 1280)), loads[11], w2),
    ):
        load.wait()
        wide = (5 - order) * 128
        product = dot(jnp.concatenate(split(plus) + split(minus), axis=0), weights[...])
        from_plus = product[0:16] + product[16:32]
        from_minus = product[32:48] + product[48:64]
        mixed_plus = from_plus[:, :wide] - from_minus[:, wide:]
        mixed_minus = from_minus[:, :wide] + from_plus[:, wide:]
        for at, degree in enumerate(range(order, 5)):
            center = degree * degree + degree
            messages[center + order] = mixed_plus[:, 128 * at : 128 * at + 128]
            messages[center - order] = mixed_minus[:, 128 * at : 128 * at + 128]
    for slot, message in messages.items():
        out_ref[slot] = (node_ref[slot].astype(F32) + message).astype(BF16)
    for slot in untouched:
        out_ref[slot] = node_ref[slot]

    stores = [
        pltpu.make_async_copy(source, target, store_sem.at[at])
        for at, (source, target) in enumerate(
            (
                (out_ref, out_hbm),
                (result_ref.at[pl.ds(0, 16)], long_hbm),
                (result_ref.at[pl.ds(16, 16)], charge_hbm),
                (pgrad_ref, pgrad_hbm),
            )
        )
    ]
    stores[0].start()

    wait_bytes(part_in, recv_sem.at[3])
    result = part[group] + jnp.sum(part_in[...], axis=0)
    result_ref[...] = result
    for axis in range(3):
        pgrad_ref[axis] = result[32 + axis : 33 + axis, 0:16]
    for store in stores[1:]:
        store.start()

    wait_bytes(table.at[pl.ds(0, 26)], halo_send)
    wait_bytes(part_in, send_sem.at[0])
    wait_bytes(all_tiles, send_sem.at[1])
    wait_bytes(summed.at[pl.ds(0, PEERS - 1)], send_sem.at[2])
    wait_bytes(part_in, send_sem.at[3])
    for store in stores:
        store.wait()


def settle(*refs):
    sources, targets, held, sems = refs[0:4], refs[4:8], refs[8:12], refs[12]
    into = [pltpu.make_async_copy(sources[at], held[at], sems.at[at]) for at in range(4)]
    out = [pltpu.make_async_copy(held[at], targets[at], sems.at[4 + at]) for at in range(4)]
    for copy in into:
        copy.start()
    for arrive, leave in zip(into, out):
        arrive.wait()
        leave.start()
    for copy in out:
        copy.wait()


def local(
    node_irreps,
    positions,
    send_list,
    neighbours,
    displacements,
    order_zero,
    order_one,
    order_two,
    reciprocal_triples,
    reciprocal_filter,
    cotangent,
):
    far = pl.BlockSpec(memory_space=pl.ANY)
    results = (
        jax.ShapeDtypeStruct((25, 16, 128), BF16),
        jax.ShapeDtypeStruct((16, 128), F32),
        jax.ShapeDtypeStruct((16, 128), F32),
        jax.ShapeDtypeStruct((3, 1, 16), F32),
    )
    held = pl.pallas_call(
        kernel,
        out_shape=results,
        in_specs=[far] * 11,
        out_specs=(far,) * 4,
        scratch_shapes=[
            pltpu.VMEM((16, 128), BF16),
            pltpu.VMEM((25, 16, 128), BF16),
            pltpu.VMEM((3, 1, 16), F32),
            pltpu.VMEM((1, 8), jnp.int32),
            pltpu.VMEM((16, 32), jnp.int32),
            pltpu.VMEM((3, 1, 512), F32),
            pltpu.VMEM((640, 640), BF16),
            pltpu.VMEM((512, 1024), BF16),
            pltpu.VMEM((384, 768), BF16),
            pltpu.VMEM((3, 1024), jnp.int32),
            pltpu.VMEM((64, 128), F32),
            pltpu.VMEM((16, 128), F32),
            pltpu.VMEM((25, 16, 128), BF16),
            pltpu.VMEM((40, 128), F32),
            pltpu.VMEM((3, 1, 16), F32),
            pltpu.VMEM((32, 16, 1280), BF16),
            pltpu.VMEM((GROUP, 40, 128), F32),
            pltpu.VMEM((8, 128), F32),
            pltpu.VMEM((PEERS, 16, 128), F32),
            pltpu.VMEM((PEERS - 1, 16, 128), F32),
            pltpu.VMEM((PEERS, 8, 128), F32),
            pltpu.VMEM((GROUP, 40, 128), F32),
            pltpu.VMEM((GROUP - 1, 40, 128), F32),
            pltpu.SemaphoreType.DMA((12,)),
            pltpu.SemaphoreType.DMA((4,)),
            pltpu.SemaphoreType.DMA,
            pltpu.SemaphoreType.DMA((2,)),
            pltpu.SemaphoreType.DMA((2,)),
            pltpu.SemaphoreType.DMA((2,)),
            pltpu.SemaphoreType.DMA((4,)),
            pltpu.SemaphoreType.DMA((4,)),
            pltpu.SemaphoreType.REGULAR,
        ],
        compiler_params=pltpu.CompilerParams(
            collective_id=0, has_side_effects=True, vmem_limit_bytes=60 * 1024 * 1024
        ),
    )(
        jnp.transpose(node_irreps[0, 0, 0], (1, 0, 2)),
        positions.reshape(3, 1, 16),
        send_list.reshape(1, 8),
        neighbours.reshape(16, 32),
        displacements.reshape(3, 1, 512),
        order_zero,
        order_one,
        order_two,
        reciprocal_triples.T,
        reciprocal_filter,
        cotangent.reshape(16, 128),
    )
    updated, long_range, charge_grad, position_grad = pl.pallas_call(
        settle,
        out_shape=results,
        in_specs=[far] * 4,
        out_specs=(far,) * 4,
        scratch_shapes=[pltpu.VMEM(held_one.shape, held_one.dtype) for held_one in results]
        + [pltpu.SemaphoreType.DMA((8,))],
        compiler_params=pltpu.CompilerParams(vmem_limit_bytes=60 * 1024 * 1024),
    )(*held)
    return (
        jnp.transpose(updated, (1, 0, 2))[None, None, None],
        long_range[None, None, None],
        charge_grad[None, None, None],
        position_grad.reshape(1, 1, 1, 3, 16),
    )


def solution(mesh):
    by_block = ("gx", "gy", "gz")
    return jax.shard_map(
        local,
        mesh=mesh,
        in_specs=(
            P(*by_block, None, None, None),
            P(*by_block, None, None),
            P(*by_block, None),
            P(*by_block, None, None),
            P(*by_block, None, None),
            P(),
            P(),
            P(),
            P(),
            P(),
            P(*by_block, None, None),
        ),
        out_specs=(
            P(*by_block, None, None, None),
            P(*by_block, None, None),
            P(*by_block, None, None),
            P(*by_block, None, None),
        ),
        check_vma=False,
    )
```

```python
import math

import jax
import jax.numpy as jnp
from jax import lax
from jax.experimental import pallas as pl
from jax.experimental.pallas import tpu as pltpu
from jax.sharding import PartitionSpec as P

MESH = pl.DeviceIdType.MESH
F32 = jnp.float32
BF16 = jnp.bfloat16

cell_length = 6.8
planar_floor = 0.25
radial_width = 64.0
atoms_total = 8192
wave_vectors = 1024
side = 8

GROUP = 16
PEERS = 32
CENTER = 13
SENT = 35
ROWS = 10

half_zero = (0, 2, 6, 12, 20, 3, 7, 13, 21)
half_one = (1, 5, 11, 19, 8, 14, 22, 4, 10, 18)
untouched = (9, 15, 16, 17, 23, 24)


x_hops, y_hops = (0, 1, 2, 1), (0, 4, 1, 3, 2, 2, 2, 2)
SIBLING = 8
mates = sorted(range(1, SIBLING), key=lambda bits: -(x_hops[bits >> 1] + bits % 2))
fellows = sorted(
    range(1, PEERS), key=lambda bits: -(y_hops[bits % 8] + (0, 2, 4, 2)[bits >> 3])
)
along_ring = [bits for bits in fellows if bits < 8]
across_rings = [bits for bits in fellows if bits % 8 == 0]


def split(values):
    high = values.astype(BF16)
    return high, (values - high.astype(F32)).astype(BF16)


def dot(a, b, dims=((1,), (0,))):
    return lax.dot_general(a, b, (dims, ((), ())), preferred_element_type=F32)


def dot3(a, b, dims=((1,), (0,))):
    a_high, a_low = split(a)
    b_high, b_low = split(b)
    return dot(a_high, b_high, dims) + (dot(a_high, b_low, dims) + dot(a_low, b_high, dims))


def cos_turns(turns):
    reduced = jnp.abs(turns - jnp.round(turns)) - 0.25
    square = reduced * reduced
    total = jnp.full_like(square, 0.0)
    for power in (13, 11, 9, 7, 5, 3, 1):
        sign = 1.0 if power % 4 == 1 else -1.0
        total = total * square + (-sign * (2.0 * math.pi) ** power / math.factorial(power))
    return total * reduced


def iota(shape, dim):
    return lax.broadcasted_iota(jnp.int32, shape, dim)


def kernel(
    node_hbm,
    pos_hbm,
    send_hbm,
    nb_hbm,
    disp_hbm,
    w0_hbm,
    w1_hbm,
    w2_hbm,
    trip_hbm,
    filt_hbm,
    cot_hbm,
    out_hbm,
    long_hbm,
    charge_hbm,
    pgrad_hbm,
    first_ref,
    node_ref,
    pos_ref,
    send_ref,
    nb_ref,
    disp_ref,
    w0,
    w1,
    w2,
    trip_ref,
    filt,
    cot_ref,
    out_ref,
    result_ref,
    pgrad_ref,
    table,
    atoms,
    trip,
    tiles,
    tiles_in,
    summed,
    part,
    pair_in,
    merged,
    part_in,
    load_sem,
    store_sem,
    halo_send,
    halo_z,
    halo_y,
    halo_x,
    send_sem,
    recv_sem,
    ring_sem,
):
    px, py, pz = lax.axis_index("gx"), lax.axis_index("gy"), lax.axis_index("gz")
    core = py % 2
    group = core * 8 + (pz // 2) * 2 + px % 2
    peer = (px // 2) * 8 + (py // 2) * 2 + pz % 2

    def turns_of(p):
        return 1 - 2 * (p % 2), 2 - 4 * ((p // 2) % 2), 4 - 8 * (p // 4)

    x_turns, y_turns, z_turns = turns_of(px), turns_of(py), turns_of(pz)
    group_turns = (x_turns[0], z_turns[1], z_turns[2], 8 * y_turns[0])
    peer_turns = (z_turns[0], y_turns[1], y_turns[2], 4 * x_turns[1], 4 * x_turns[2])

    def turned(start, bits, steps):
        for at, step in enumerate(steps):
            if (bits >> at) % 2:
                start = start + step
        return start

    def mate(bits):
        return turned(group, bits, group_turns), (
            turned(px, bits & 1, x_turns),
            turned(py, bits >> 3, y_turns),
            turned(pz, (bits >> 1 & 3) << 1, z_turns),
        )

    def fellow(bits):
        return turned(peer, bits, peer_turns), (
            turned(px, (bits >> 3) << 1, x_turns),
            turned(py, (bits >> 1 & 3) << 1, y_turns),
            turned(pz, bits & 1, z_turns),
        )

    around_x = ((px + 1) % side, py, pz), ((px + side - 1) % side, py, pz)
    around_y = (px, (py + 1) % side, pz), (px, (py + side - 1) % side, pz)
    around_z = (px, py, (pz + 1) % side), (px, py, (pz + side - 1) % side)

    def wait_bytes(ref, sem):
        pltpu.make_async_copy(ref, ref, sem).wait()

    slab = pl.multiple_of(group * 64, 64)
    loads = [
        pltpu.make_async_copy(source, target, load_sem.at[at])
        for at, (source, target) in enumerate(
            (
                (node_hbm.at[0], first_ref),
                (cot_hbm, cot_ref),
                (pos_hbm, pos_ref),
                (node_hbm, node_ref),
                (send_hbm, send_ref),
                (trip_hbm, trip_ref),
                (disp_hbm, disp_ref),
                (nb_hbm, nb_ref),
                (filt_hbm.at[pl.ds(slab, 64), :], filt),
                (w0_hbm, w0),
                (w1_hbm, w1),
                (w2_hbm, w2),
            )
        )
    ]
    for load in loads:
        load.start()

    barrier = pltpu.get_barrier_semaphore()

    def greet(device):
        pl.semaphore_signal(barrier, inc=1, device_id=device, device_id_type=MESH)

    for bits in along_ring + across_rings:
        greet(fellow(bits)[1])
    for device in around_z + around_y + around_x:
        greet(device)
    for bits in mates + [SIBLING]:
        greet(mate(bits)[1])

    for load in loads[:3]:
        load.wait()
    atoms[group, 0:16, :] = first_ref[...].astype(F32)
    atoms[group, 16:32, :] = cot_ref[...]
    trip[...] = jnp.zeros((8, 128), F32)
    for axis, index in enumerate((px, py, pz)):
        corner = cell_length * index.astype(F32)
        trip[axis : axis + 1, 0:16] = (pos_ref[axis] + corner) / (cell_length * side)
    atoms[group, 32:40, :] = pltpu.roll(trip[...], 16 * (group % 8), axis=1)

    pl.semaphore_wait(barrier, len(mates) + 1 + len(along_ring) + len(across_rings) + 6)

    for bits in mates:
        pltpu.make_async_remote_copy(
            src_ref=atoms.at[group, pl.ds(0, SENT)],
            dst_ref=atoms.at[group, pl.ds(0, SENT)],
            send_sem=send_sem.at[0],
            recv_sem=recv_sem.at[0],
            device_id=mate(bits)[1],
            device_id_type=MESH,
        ).start()

    for bits in across_rings:
        pl.semaphore_signal(
            ring_sem, inc=1, device_id=fellow(bits)[1], device_id_type=MESH
        )

    for load in loads[3:5]:
        load.wait()
    own_zero = jnp.concatenate(
        [node_ref[s] for s in half_zero] + [jnp.zeros((16, 128), BF16)], axis=1
    )
    own_one = jnp.concatenate([node_ref[s] for s in half_one], axis=1)
    sent = jnp.sum(
        jnp.where(
            iota((16, 8), 0) % 8 == iota((16, 8), 1),
            jnp.broadcast_to(send_ref[...], (16, 8)).astype(F32),
            0.0,
        ),
        axis=1,
        keepdims=True,
    )
    chosen = jnp.where(iota((16, 16), 1).astype(F32) == sent, 1.0, 0.0).astype(BF16)
    upper = iota((16, 1280), 0) < 8
    table[CENTER] = jnp.where(upper, dot(chosen, own_zero), dot(chosen, own_one)).astype(BF16)

    def pass_on(first, count, to, device, sem):
        pltpu.make_async_remote_copy(
            src_ref=table.at[pl.ds(first, count)],
            dst_ref=table.at[pl.ds(to, count)],
            send_sem=halo_send,
            recv_sem=sem,
            device_id=device,
            device_id_type=MESH,
        ).start()

    def along_z(first, count):
        pass_on(first, count, first - 1, around_z[0], halo_z.at[0])
        pass_on(first, count, first + 1, around_z[1], halo_z.at[1])

    def along_y(first, count):
        pass_on(first, count, first - 3, around_y[0], halo_y.at[0])
        pass_on(first, count, first + 3, around_y[1], halo_y.at[1])

    def along_x(first, count):
        pass_on(first, count, first - 9, around_x[0], halo_x.at[0])
        pass_on(first, count, first + 9, around_x[1], halo_x.at[1])

    along_z(CENTER, 1)
    along_y(CENTER, 1)
    along_x(CENTER, 1)

    own_zero_wide, own_one_wide = own_zero.astype(F32), own_one.astype(F32)
    for part_of in range(2):
        rows = slice(8 * part_of, 8 * part_of + 8)
        table[27 + part_of] = jnp.concatenate(
            [own_zero_wide[rows], own_one_wide[rows]], axis=0
        ).astype(BF16)
    for spare in range(29, 32):
        table[spare] = jnp.zeros((16, 1280), BF16)

    for load in loads[5:8]:
        load.wait()
    block = trip_ref[:, pl.ds(pl.multiple_of((group // 2) * 128, 128), 128)].astype(F32)
    trip[...] = jnp.zeros((8, 128), F32)
    trip[0:3, :] = block
    block = trip[...]
    triples = jnp.where(
        iota((8, 128), 1) // 64 == group % 2, block, pltpu.roll(block, 64, axis=1)
    )
    triples_down = triples.T

    d0, d1, d2 = disp_ref[0], disp_ref[1], disp_ref[2]
    radial = jnp.exp(-(d0 * d0 + d1 * d1 + d2 * d2) / radial_width) / math.sqrt(32)
    planar = jnp.sqrt(d0 * d0 + d1 * d1 + planar_floor)
    cos_one, sin_one = d0 / planar, d1 / planar
    cos_two, sin_two = cos_one * cos_one - sin_one * sin_one, 2.0 * cos_one * sin_one
    edge_weights = (
        radial,
        radial * (cos_one * cos_one + sin_one * sin_one),
        radial * (cos_two * cos_two + sin_two * sin_two),
    )
    of_atom = iota((16, 512), 1) // 32 == iota((16, 512), 0)
    repeat = jnp.where(iota((32, 512), 1) % 32 == iota((32, 512), 0), 1.0, 0.0).astype(BF16)
    named = dot(nb_ref[...].astype(F32).astype(BF16), repeat)
    named = jnp.sum(jnp.where(of_atom, named, 0.0), axis=0, keepdims=True)
    row = iota((512, 128), 0)
    place_of, atom_of = row // 16, row % 16
    listed = jnp.where(
        place_of < 27, 16 + 8 * place_of + atom_of, 8 * (place_of - 27) + atom_of
    )
    listed = jnp.where((atom_of < 8) & (place_of < 29), listed, -1).astype(F32)
    hits = jnp.concatenate(
        [
            jnp.where(named[:, 128 * b : 128 * b + 128] == listed, 1.0, 0.0).astype(BF16)
            for b in range(4)
        ],
        axis=1,
    )
    weight_rows = []
    for weight in edge_weights:
        for piece in split(jnp.where(of_atom, jnp.broadcast_to(weight, (16, 512)), 0.0)):
            weight_rows.append(piece)
    gathered = dot(jnp.concatenate(weight_rows, axis=0), hits, ((1,), (1,)))
    by_order = [gathered[32 * m : 32 * m + 16] + gathered[32 * m + 16 : 32 * m + 32] for m in range(3)]
    mixers = []
    for values in (
        by_order[0],
        by_order[1],
        pltpu.roll(by_order[1], 8, axis=1),
        pltpu.roll(by_order[2], 8, axis=1),
    ):
        mixers.extend(split(values))
    mixers = jnp.concatenate(mixers, axis=0)

    wait_bytes(atoms.at[pl.ds(0, 7), pl.ds(0, SENT)], recv_sem.at[0])
    ours = pl.ds(core * 8, 8)
    pltpu.make_async_remote_copy(
        src_ref=atoms.at[ours, pl.ds(0, SENT)],
        dst_ref=atoms.at[ours, pl.ds(0, SENT)],
        send_sem=send_sem.at[4],
        recv_sem=recv_sem.at[4],
        device_id=mate(SIBLING)[1],
        device_id_type=MESH,
    ).start()
    wait_bytes(atoms.at[pl.ds(0, 8), pl.ds(0, SENT)], recv_sem.at[4])
    charges = atoms[:, 0:16, :].reshape(256, 128)
    grad_input = atoms[:, 16:32, :].reshape(256, 128)
    places = jnp.concatenate(
        [jnp.sum(atoms[low : low + 8, 32:35, :], axis=0) for low in (0, 8)], axis=1
    )
    turns = (
        triples_down[:, 0:1] * places[0:1, :]
        + triples_down[:, 1:2] * places[1:2, :]
        + triples_down[:, 2:3] * places[2:3, :]
    )
    is_sine = iota((128, 256), 0) >= 64
    waves = cos_turns(turns - jnp.where(is_sine, 0.25, 0.0))
    waves_high, waves_low = split(waves)
    charges_half = charges.astype(BF16)
    grad_high, grad_low = split(grad_input)
    raw = dot(waves_high, charges_half) + dot(waves_low, charges_half)
    response = dot(waves_high, grad_high) + (
        dot(waves_high, grad_low) + dot(waves_low, grad_high)
    )
    waves_across = waves.T
    tiles[0:16, 0:8, :] = raw.reshape(16, 8, 128)
    tiles[16:32, 0:8, :] = response.reshape(16, 8, 128)
    plane = jnp.sum(waves_across, axis=0, keepdims=True)
    total_charge = jnp.sum(charges, axis=0, keepdims=True)
    extra = jnp.concatenate([plane, total_charge, jnp.zeros((6, 128), F32)], axis=0)
    tiles[:, 8:16, :] = jnp.broadcast_to(extra, (PEERS, 8, 128))

    pl.semaphore_wait(ring_sem, len(across_rings))

    for bits in fellows:
        other, device = fellow(bits)
        pltpu.make_async_remote_copy(
            src_ref=tiles.at[other, pl.ds(0, ROWS)],
            dst_ref=tiles_in.at[bits - 1, pl.ds(0, ROWS)],
            send_sem=send_sem.at[1],
            recv_sem=recv_sem.at[1],
            device_id=device,
            device_id_type=MESH,
        ).start()

    wait_bytes(table.at[12], halo_z.at[0])
    wait_bytes(table.at[14], halo_z.at[1])
    for piece in (12, 14):
        along_y(piece, 1)
    for piece in (12, 14):
        along_x(piece, 1)

    all_tiles = tiles_in.at[:, pl.ds(0, ROWS), :]
    wait_bytes(all_tiles, recv_sem.at[1])
    whole = tiles[peer, 0:ROWS, :] + jnp.sum(tiles_in[:, 0:ROWS, :], axis=0)
    summed[peer] = whole[0:8]
    plane, total_charge = whole[8:9], whole[9:10]
    for bits in fellows:
        pltpu.make_async_remote_copy(
            src_ref=summed.at[peer],
            dst_ref=summed.at[peer],
            send_sem=send_sem.at[2],
            recv_sem=recv_sem.at[2],
            device_id=fellow(bits)[1],
            device_id_type=MESH,
        ).start()

    wait_bytes(table.at[pl.ds(9, 3)], halo_y.at[0])
    along_x(9, 3)
    wait_bytes(table.at[pl.ds(15, 3)], halo_y.at[1])
    along_x(15, 3)

    scale = 1.0 / math.sqrt(atoms_total * wave_vectors)
    loads[8].wait()
    wait_bytes(summed.at[pl.ds(0, PEERS - 1)], recv_sem.at[2])
    mean_charge = total_charge / atoms_total
    plane_down = jnp.broadcast_to(plane, (8, 128)).T[:, 0:1]
    factor = filt[...] * scale
    factor = jnp.concatenate([factor, factor], axis=0)
    filtered = factor * (summed[0:16].reshape(128, 128) - plane_down * mean_charge)
    filtered_response = factor * summed[16:32].reshape(128, 128)
    long_part = dot3(waves_across, filtered)
    charge_part = dot3(waves_across - plane / atoms_total, filtered_response)

    def swapped(values):
        return jnp.concatenate([values[64:], values[:64]], axis=0)

    both = jnp.concatenate([swapped(filtered), swapped(filtered_response)], axis=1)
    sides = jnp.concatenate([grad_input, charges - mean_charge], axis=1)
    phase_grad = waves * dot3(both, sides, ((1,), (1,)))
    signed = jnp.where(iota((8, 128), 1) < 64, triples, -triples).astype(BF16)
    phase_high, phase_low = split(phase_grad)
    pgrad = (dot(signed, phase_high) + dot(signed, phase_low)) * (
        2.0 * math.pi / (cell_length * side)
    )
    part[:, 0:16, :] = long_part.reshape(GROUP, 16, 128)
    part[:, 16:32, :] = charge_part.reshape(GROUP, 16, 128)
    for device in range(GROUP):
        low = 128 * (device // 8)
        values = pgrad[:, low : low + 128]
        if device % 8:
            values = pltpu.roll(values, 128 - 16 * (device % 8), axis=1)
        part[device, 32:40, :] = values

    theirs = pl.ds(8 - core * 8, 8)
    pltpu.make_async_remote_copy(
        src_ref=part.at[theirs, pl.ds(0, SENT)],
        dst_ref=pair_in.at[:, pl.ds(0, SENT)],
        send_sem=send_sem.at[5],
        recv_sem=recv_sem.at[5],
        device_id=mate(SIBLING)[1],
        device_id_type=MESH,
    ).start()
    wait_bytes(pair_in.at[:, pl.ds(0, SENT)], recv_sem.at[5])
    merged[:, 0:SENT, :] = part[ours, 0:SENT, :] + pair_in[:, 0:SENT, :]
    own = group % 8
    for bits in mates:
        other, device = mate(bits)
        pltpu.make_async_remote_copy(
            src_ref=merged.at[other % 8, pl.ds(0, SENT)],
            dst_ref=part_in.at[bits - 1, pl.ds(0, SENT)],
            send_sem=send_sem.at[3],
            recv_sem=recv_sem.at[3],
            device_id=device,
            device_id_type=MESH,
        ).start()

    wait_bytes(table.at[pl.ds(0, 9)], halo_x.at[0])
    wait_bytes(table.at[pl.ds(18, 9)], halo_x.at[1])
    collected = dot(mixers, table[...].reshape(512, 1280))

    def pair(first, lanes):
        return collected[first : first + 16, lanes] + collected[first + 16 : first + 32, lanes]

    loads[9].wait()
    mixed = dot(jnp.concatenate(split(pair(0, slice(0, 640))), axis=0), w0[...])
    mixed = mixed[0:16] + mixed[16:32]
    messages = {l * l + l: mixed[:, 128 * l : 128 * l + 128] for l in range(5)}
    for order, plus, minus, load, weights in (
        (1, pair(32, slice(640, 1152)), pair(64, slice(0, 512)), loads[10], w1),
        (2, pair(96, slice(512, 896)), pair(96, slice(896, 1280)), loads[11], w2),
    ):
        load.wait()
        wide = (5 - order) * 128
        product = dot(jnp.concatenate(split(plus) + split(minus), axis=0), weights[...])
        from_plus = product[0:16] + product[16:32]
        from_minus = product[32:48] + product[48:64]
        mixed_plus = from_plus[:, :wide] - from_minus[:, wide:]
        mixed_minus = from_minus[:, :wide] + from_plus[:, wide:]
        for at, degree in enumerate(range(order, 5)):
            center = degree * degree + degree
            messages[center + order] = mixed_plus[:, 128 * at : 128 * at + 128]
            messages[center - order] = mixed_minus[:, 128 * at : 128 * at + 128]
    for slot, message in messages.items():
        out_ref[slot] = (node_ref[slot].astype(F32) + message).astype(BF16)
    for slot in untouched:
        out_ref[slot] = node_ref[slot]

    stores = [
        pltpu.make_async_copy(source, target, store_sem.at[at])
        for at, (source, target) in enumerate(
            (
                (out_ref, out_hbm),
                (result_ref.at[pl.ds(0, 16)], long_hbm),
                (result_ref.at[pl.ds(16, 16)], charge_hbm),
                (pgrad_ref, pgrad_hbm),
            )
        )
    ]
    stores[0].start()

    all_parts = part_in.at[:, pl.ds(0, SENT), :]
    wait_bytes(all_parts, recv_sem.at[3])
    result = merged[own, 0:SENT, :] + jnp.sum(part_in[:, 0:SENT, :], axis=0)
    result_ref[0:32] = result[0:32]
    for axis in range(3):
        pgrad_ref[axis] = result[32 + axis : 33 + axis, 0:16]
    for store in stores[1:]:
        store.start()

    wait_bytes(table.at[pl.ds(0, 26)], halo_send)
    wait_bytes(all_parts, send_sem.at[0])
    wait_bytes(pair_in.at[:, pl.ds(0, SENT)], send_sem.at[4])
    wait_bytes(all_tiles, send_sem.at[1])
    wait_bytes(summed.at[pl.ds(0, PEERS - 1)], send_sem.at[2])
    wait_bytes(all_parts, send_sem.at[3])
    wait_bytes(pair_in.at[:, pl.ds(0, SENT)], send_sem.at[5])
    for store in stores:
        store.wait()


def settle(*refs):
    sources, targets, held, sems = refs[0:4], refs[4:8], refs[8:12], refs[12]
    into = [pltpu.make_async_copy(sources[at], held[at], sems.at[at]) for at in range(4)]
    out = [pltpu.make_async_copy(held[at], targets[at], sems.at[4 + at]) for at in range(4)]
    for copy in into:
        copy.start()
    for arrive, leave in zip(into, out):
        arrive.wait()
        leave.start()
    for copy in out:
        copy.wait()


def local(
    node_irreps,
    positions,
    send_list,
    neighbours,
    displacements,
    order_zero,
    order_one,
    order_two,
    reciprocal_triples,
    reciprocal_filter,
    cotangent,
):
    far = pl.BlockSpec(memory_space=pl.ANY)
    results = (
        jax.ShapeDtypeStruct((25, 16, 128), BF16),
        jax.ShapeDtypeStruct((16, 128), F32),
        jax.ShapeDtypeStruct((16, 128), F32),
        jax.ShapeDtypeStruct((3, 1, 16), F32),
    )
    held = pl.pallas_call(
        kernel,
        out_shape=results,
        in_specs=[far] * 11,
        out_specs=(far,) * 4,
        scratch_shapes=[
            pltpu.VMEM((16, 128), BF16),
            pltpu.VMEM((25, 16, 128), BF16),
            pltpu.VMEM((3, 1, 16), F32),
            pltpu.VMEM((1, 8), jnp.int32),
            pltpu.VMEM((16, 32), jnp.int32),
            pltpu.VMEM((3, 1, 512), F32),
            pltpu.VMEM((640, 640), BF16),
            pltpu.VMEM((512, 1024), BF16),
            pltpu.VMEM((384, 768), BF16),
            pltpu.VMEM((3, 1024), jnp.int32),
            pltpu.VMEM((64, 128), F32),
            pltpu.VMEM((16, 128), F32),
            pltpu.VMEM((25, 16, 128), BF16),
            pltpu.VMEM((40, 128), F32),
            pltpu.VMEM((3, 1, 16), F32),
            pltpu.VMEM((32, 16, 1280), BF16),
            pltpu.VMEM((GROUP, 40, 128), F32),
            pltpu.VMEM((8, 128), F32),
            pltpu.VMEM((PEERS, 16, 128), F32),
            pltpu.VMEM((PEERS - 1, 16, 128), F32),
            pltpu.VMEM((PEERS, 8, 128), F32),
            pltpu.VMEM((GROUP, 40, 128), F32),
            pltpu.VMEM((8, 40, 128), F32),
            pltpu.VMEM((8, 40, 128), F32),
            pltpu.VMEM((7, 40, 128), F32),
            pltpu.SemaphoreType.DMA((12,)),
            pltpu.SemaphoreType.DMA((4,)),
            pltpu.SemaphoreType.DMA,
            pltpu.SemaphoreType.DMA((2,)),
            pltpu.SemaphoreType.DMA((2,)),
            pltpu.SemaphoreType.DMA((2,)),
            pltpu.SemaphoreType.DMA((6,)),
            pltpu.SemaphoreType.DMA((6,)),
            pltpu.SemaphoreType.REGULAR,
        ],
        compiler_params=pltpu.CompilerParams(
            collective_id=0, has_side_effects=True, vmem_limit_bytes=60 * 1024 * 1024
        ),
    )(
        jnp.transpose(node_irreps[0, 0, 0], (1, 0, 2)),
        positions.reshape(3, 1, 16),
        send_list.reshape(1, 8),
        neighbours.reshape(16, 32),
        displacements.reshape(3, 1, 512),
        order_zero,
        order_one,
        order_two,
        reciprocal_triples.T,
        reciprocal_filter,
        cotangent.reshape(16, 128),
    )
    updated, long_range, charge_grad, position_grad = pl.pallas_call(
        settle,
        out_shape=results,
        in_specs=[far] * 4,
        out_specs=(far,) * 4,
        scratch_shapes=[pltpu.VMEM(held_one.shape, held_one.dtype) for held_one in results]
        + [pltpu.SemaphoreType.DMA((8,))],
        compiler_params=pltpu.CompilerParams(vmem_limit_bytes=60 * 1024 * 1024),
    )(*held)
    return (
        jnp.transpose(updated, (1, 0, 2))[None, None, None],
        long_range[None, None, None],
        charge_grad[None, None, None],
        position_grad.reshape(1, 1, 1, 3, 16),
    )


def solution(mesh):
    by_block = ("gx", "gy", "gz")
    return jax.shard_map(
        local,
        mesh=mesh,
        in_specs=(
            P(*by_block, None, None, None),
            P(*by_block, None, None),
            P(*by_block, None),
            P(*by_block, None, None),
            P(*by_block, None, None),
            P(),
            P(),
            P(),
            P(),
            P(),
            P(*by_block, None, None),
        ),
        out_specs=(
            P(*by_block, None, None, None),
            P(*by_block, None, None),
            P(*by_block, None, None),
            P(*by_block, None, None),
        ),
        check_vma=False,
    )
```

```python
import math

import jax
import jax.numpy as jnp
from jax import lax
from jax.experimental import pallas as pl
from jax.experimental.pallas import tpu as pltpu
from jax.sharding import PartitionSpec as P

MESH = pl.DeviceIdType.MESH
F32 = jnp.float32
BF16 = jnp.bfloat16

cell_length = 6.8
planar_floor = 0.25
radial_width = 64.0
atoms_total = 8192
wave_vectors = 1024
side = 8

GROUP = 16
PEERS = 32
CENTER = 13
SENT = 35
ROWS = 10

half_zero = (0, 2, 6, 12, 20, 3, 7, 13, 21)
half_one = (1, 5, 11, 19, 8, 14, 22, 4, 10, 18)
untouched = (9, 15, 16, 17, 23, 24)


x_hops, y_hops = (0, 1, 2, 1), (0, 4, 1, 3, 2, 2, 2, 2)
SIBLING = 8
mates = sorted(range(1, SIBLING), key=lambda bits: -(x_hops[bits >> 1] + bits % 2))
fellows = sorted(
    range(1, PEERS), key=lambda bits: -(y_hops[bits % 8] + (0, 2, 4, 2)[bits >> 3])
)
along_ring = [bits for bits in fellows if bits < 8]
across_rings = [bits for bits in fellows if bits % 8 == 0]


def split(values):
    high = values.astype(BF16)
    return high, (values - high.astype(F32)).astype(BF16)


def dot(a, b, dims=((1,), (0,))):
    return lax.dot_general(a, b, (dims, ((), ())), preferred_element_type=F32)


def dot3(a_split, b_split, dims=((1,), (0,))):
    a_high, a_low = a_split
    b_high, b_low = b_split
    return dot(a_high, b_high, dims) + (dot(a_high, b_low, dims) + dot(a_low, b_high, dims))


def cos_turns(turns):
    reduced = jnp.abs(turns - jnp.round(turns)) - 0.25
    square = reduced * reduced
    total = jnp.full_like(square, 0.0)
    for power in (13, 11, 9, 7, 5, 3, 1):
        sign = 1.0 if power % 4 == 1 else -1.0
        total = total * square + (-sign * (2.0 * math.pi) ** power / math.factorial(power))
    return total * reduced


def iota(shape, dim):
    return lax.broadcasted_iota(jnp.int32, shape, dim)


def kernel(
    node_hbm,
    pos_hbm,
    send_hbm,
    nb_hbm,
    disp_hbm,
    w0_hbm,
    w1_hbm,
    w2_hbm,
    trip_hbm,
    filt_hbm,
    cot_hbm,
    out_hbm,
    long_hbm,
    charge_hbm,
    pgrad_hbm,
    first_ref,
    node_ref,
    pos_ref,
    send_ref,
    nb_ref,
    disp_ref,
    w0,
    w1,
    w2,
    trip_ref,
    filt,
    cot_ref,
    out_ref,
    result_ref,
    pgrad_ref,
    table,
    atoms,
    trip,
    tiles,
    tiles_in,
    summed,
    part,
    pair_in,
    merged,
    part_in,
    load_sem,
    store_sem,
    halo_send,
    halo_z,
    halo_y,
    halo_x,
    send_sem,
    recv_sem,
    ring_sem,
):
    px, py, pz = lax.axis_index("gx"), lax.axis_index("gy"), lax.axis_index("gz")
    core = py % 2
    group = core * 8 + (pz // 2) * 2 + px % 2
    peer = (px // 2) * 8 + (py // 2) * 2 + pz % 2

    def turns_of(p):
        return 1 - 2 * (p % 2), 2 - 4 * ((p // 2) % 2), 4 - 8 * (p // 4)

    x_turns, y_turns, z_turns = turns_of(px), turns_of(py), turns_of(pz)
    group_turns = (x_turns[0], z_turns[1], z_turns[2], 8 * y_turns[0])
    peer_turns = (z_turns[0], y_turns[1], y_turns[2], 4 * x_turns[1], 4 * x_turns[2])

    def turned(start, bits, steps):
        for at, step in enumerate(steps):
            if (bits >> at) % 2:
                start = start + step
        return start

    def mate(bits):
        return turned(group, bits, group_turns), (
            turned(px, bits & 1, x_turns),
            turned(py, bits >> 3, y_turns),
            turned(pz, (bits >> 1 & 3) << 1, z_turns),
        )

    def fellow(bits):
        return turned(peer, bits, peer_turns), (
            turned(px, (bits >> 3) << 1, x_turns),
            turned(py, (bits >> 1 & 3) << 1, y_turns),
            turned(pz, bits & 1, z_turns),
        )

    around_x = ((px + 1) % side, py, pz), ((px + side - 1) % side, py, pz)
    around_y = (px, (py + 1) % side, pz), (px, (py + side - 1) % side, pz)
    around_z = (px, py, (pz + 1) % side), (px, py, (pz + side - 1) % side)

    def wait_bytes(ref, sem):
        pltpu.make_async_copy(ref, ref, sem).wait()

    slab = pl.multiple_of(group * 64, 64)
    loads = [
        pltpu.make_async_copy(source, target, load_sem.at[at])
        for at, (source, target) in enumerate(
            (
                (node_hbm.at[0], first_ref),
                (cot_hbm, cot_ref),
                (pos_hbm, pos_ref),
                (node_hbm, node_ref),
                (send_hbm, send_ref),
                (trip_hbm, trip_ref),
                (disp_hbm, disp_ref),
                (nb_hbm, nb_ref),
                (filt_hbm.at[pl.ds(slab, 64), :], filt),
                (w0_hbm, w0),
                (w1_hbm, w1),
                (w2_hbm, w2),
            )
        )
    ]
    for load in loads:
        load.start()

    barrier = pltpu.get_barrier_semaphore()

    def greet(device):
        pl.semaphore_signal(barrier, inc=1, device_id=device, device_id_type=MESH)

    for bits in along_ring + across_rings:
        greet(fellow(bits)[1])
    for device in around_z + around_y + around_x:
        greet(device)
    for bits in mates + [SIBLING]:
        greet(mate(bits)[1])

    for load in loads[:3]:
        load.wait()
    atoms[group, 0:16, :] = first_ref[...].astype(F32)
    atoms[group, 16:32, :] = cot_ref[...]
    trip[...] = jnp.zeros((8, 128), F32)
    for axis, index in enumerate((px, py, pz)):
        corner = cell_length * index.astype(F32)
        trip[axis : axis + 1, 0:16] = (pos_ref[axis] + corner) / (cell_length * side)
    atoms[group, 32:40, :] = pltpu.roll(trip[...], 16 * (group % 8), axis=1)

    pl.semaphore_wait(barrier, len(mates) + 1 + len(along_ring) + len(across_rings) + 6)

    for bits in mates:
        pltpu.make_async_remote_copy(
            src_ref=atoms.at[group, pl.ds(0, SENT)],
            dst_ref=atoms.at[group, pl.ds(0, SENT)],
            send_sem=send_sem.at[0],
            recv_sem=recv_sem.at[0],
            device_id=mate(bits)[1],
            device_id_type=MESH,
        ).start()

    for bits in across_rings:
        pl.semaphore_signal(
            ring_sem, inc=1, device_id=fellow(bits)[1], device_id_type=MESH
        )

    for load in loads[3:5]:
        load.wait()
    own_zero = jnp.concatenate(
        [node_ref[s] for s in half_zero] + [jnp.zeros((16, 128), BF16)], axis=1
    )
    own_one = jnp.concatenate([node_ref[s] for s in half_one], axis=1)
    sent = jnp.sum(
        jnp.where(
            iota((16, 8), 0) % 8 == iota((16, 8), 1),
            jnp.broadcast_to(send_ref[...], (16, 8)).astype(F32),
            0.0,
        ),
        axis=1,
        keepdims=True,
    )
    chosen = jnp.where(iota((16, 16), 1).astype(F32) == sent, 1.0, 0.0).astype(BF16)
    upper = iota((16, 1280), 0) < 8
    table[CENTER] = jnp.where(upper, dot(chosen, own_zero), dot(chosen, own_one)).astype(BF16)

    def pass_on(first, count, to, device, sem):
        pltpu.make_async_remote_copy(
            src_ref=table.at[pl.ds(first, count)],
            dst_ref=table.at[pl.ds(to, count)],
            send_sem=halo_send,
            recv_sem=sem,
            device_id=device,
            device_id_type=MESH,
        ).start()

    def along_z(first, count):
        pass_on(first, count, first - 1, around_z[0], halo_z.at[0])
        pass_on(first, count, first + 1, around_z[1], halo_z.at[1])

    def along_y(first, count):
        pass_on(first, count, first - 3, around_y[0], halo_y.at[0])
        pass_on(first, count, first + 3, around_y[1], halo_y.at[1])

    def along_x(first, count):
        pass_on(first, count, first - 9, around_x[0], halo_x.at[0])
        pass_on(first, count, first + 9, around_x[1], halo_x.at[1])

    along_z(CENTER, 1)
    along_y(CENTER, 1)
    along_x(CENTER, 1)

    own_zero_wide, own_one_wide = own_zero.astype(F32), own_one.astype(F32)
    for part_of in range(2):
        rows = slice(8 * part_of, 8 * part_of + 8)
        table[27 + part_of] = jnp.concatenate(
            [own_zero_wide[rows], own_one_wide[rows]], axis=0
        ).astype(BF16)
    for spare in range(29, 32):
        table[spare] = jnp.zeros((16, 1280), BF16)

    for load in loads[5:8]:
        load.wait()
    block = trip_ref[:, pl.ds(pl.multiple_of((group // 2) * 128, 128), 128)].astype(F32)
    trip[...] = jnp.zeros((8, 128), F32)
    trip[0:3, :] = block
    block = trip[...]
    triples = jnp.where(
        iota((8, 128), 1) // 64 == group % 2, block, pltpu.roll(block, 64, axis=1)
    )
    triples_down = triples.T

    d0, d1, d2 = disp_ref[0], disp_ref[1], disp_ref[2]
    radial = jnp.exp(-(d0 * d0 + d1 * d1 + d2 * d2) / radial_width) / math.sqrt(32)
    planar = jnp.sqrt(d0 * d0 + d1 * d1 + planar_floor)
    cos_one, sin_one = d0 / planar, d1 / planar
    cos_two, sin_two = cos_one * cos_one - sin_one * sin_one, 2.0 * cos_one * sin_one
    edge_weights = (
        radial,
        radial * (cos_one * cos_one + sin_one * sin_one),
        radial * (cos_two * cos_two + sin_two * sin_two),
    )
    of_atom = iota((16, 512), 1) // 32 == iota((16, 512), 0)
    repeat = jnp.where(iota((32, 512), 1) % 32 == iota((32, 512), 0), 1.0, 0.0).astype(BF16)
    named = dot(nb_ref[...].astype(F32).astype(BF16), repeat)
    named = jnp.sum(jnp.where(of_atom, named, 0.0), axis=0, keepdims=True)
    row = iota((512, 128), 0)
    place_of, atom_of = row // 16, row % 16
    listed = jnp.where(
        place_of < 27, 16 + 8 * place_of + atom_of, 8 * (place_of - 27) + atom_of
    )
    listed = jnp.where((atom_of < 8) & (place_of < 29), listed, -1).astype(F32)
    hits = jnp.concatenate(
        [
            jnp.where(named[:, 128 * b : 128 * b + 128] == listed, 1.0, 0.0).astype(BF16)
            for b in range(4)
        ],
        axis=1,
    )
    weight_rows = []
    for weight in edge_weights:
        for piece in split(jnp.where(of_atom, jnp.broadcast_to(weight, (16, 512)), 0.0)):
            weight_rows.append(piece)
    gathered = dot(jnp.concatenate(weight_rows, axis=0), hits, ((1,), (1,)))
    by_order = [gathered[32 * m : 32 * m + 16] + gathered[32 * m + 16 : 32 * m + 32] for m in range(3)]
    mixers = []
    for values in (
        by_order[0],
        by_order[1],
        pltpu.roll(by_order[1], 8, axis=1),
        pltpu.roll(by_order[2], 8, axis=1),
    ):
        mixers.extend(split(values))
    mixers = jnp.concatenate(mixers, axis=0)

    wait_bytes(atoms.at[pl.ds(0, 7), pl.ds(0, SENT)], recv_sem.at[0])
    ours = pl.ds(core * 8, 8)
    pltpu.make_async_remote_copy(
        src_ref=atoms.at[ours, pl.ds(0, SENT)],
        dst_ref=atoms.at[ours, pl.ds(0, SENT)],
        send_sem=send_sem.at[4],
        recv_sem=recv_sem.at[4],
        device_id=mate(SIBLING)[1],
        device_id_type=MESH,
    ).start()
    wait_bytes(atoms.at[pl.ds(0, 8), pl.ds(0, SENT)], recv_sem.at[4])
    charges = atoms[:, 0:16, :].reshape(256, 128)
    grad_input = atoms[:, 16:32, :].reshape(256, 128)
    places = jnp.concatenate(
        [jnp.sum(atoms[low : low + 8, 32:35, :], axis=0) for low in (0, 8)], axis=1
    )
    turns = (
        triples_down[:, 0:1] * places[0:1, :]
        + triples_down[:, 1:2] * places[1:2, :]
        + triples_down[:, 2:3] * places[2:3, :]
    )
    is_sine = iota((128, 256), 0) >= 64
    waves = cos_turns(turns - jnp.where(is_sine, 0.25, 0.0))
    waves_high, waves_low = split(waves)
    charges_half = charges.astype(BF16)
    grad_high, grad_low = split(grad_input)
    raw = dot(waves_high, charges_half) + dot(waves_low, charges_half)
    response = dot(waves_high, grad_high) + (
        dot(waves_high, grad_low) + dot(waves_low, grad_high)
    )
    waves_across = waves.T
    tiles[0:16, 0:8, :] = raw.reshape(16, 8, 128)
    tiles[16:32, 0:8, :] = response.reshape(16, 8, 128)
    plane = jnp.sum(waves_across, axis=0, keepdims=True)
    total_charge = jnp.sum(charges, axis=0, keepdims=True)
    extra = jnp.concatenate([plane, total_charge, jnp.zeros((6, 128), F32)], axis=0)
    tiles[:, 8:16, :] = jnp.broadcast_to(extra, (PEERS, 8, 128))

    pl.semaphore_wait(ring_sem, len(across_rings))

    for bits in fellows:
        other, device = fellow(bits)
        pltpu.make_async_remote_copy(
            src_ref=tiles.at[other, pl.ds(0, ROWS)],
            dst_ref=tiles_in.at[bits - 1, pl.ds(0, ROWS)],
            send_sem=send_sem.at[1],
            recv_sem=recv_sem.at[1],
            device_id=device,
            device_id_type=MESH,
        ).start()

    wait_bytes(table.at[12], halo_z.at[0])
    wait_bytes(table.at[14], halo_z.at[1])
    for piece in (12, 14):
        along_y(piece, 1)
    for piece in (12, 14):
        along_x(piece, 1)

    all_tiles = tiles_in.at[:, pl.ds(0, ROWS), :]
    wait_bytes(all_tiles, recv_sem.at[1])
    whole = tiles[peer, 0:ROWS, :] + jnp.sum(tiles_in[:, 0:ROWS, :], axis=0)
    summed[peer] = whole[0:8]
    plane, total_charge = whole[8:9], whole[9:10]
    for bits in fellows:
        pltpu.make_async_remote_copy(
            src_ref=summed.at[peer],
            dst_ref=summed.at[peer],
            send_sem=send_sem.at[2],
            recv_sem=recv_sem.at[2],
            device_id=fellow(bits)[1],
            device_id_type=MESH,
        ).start()

    wait_bytes(table.at[pl.ds(9, 3)], halo_y.at[0])
    along_x(9, 3)
    wait_bytes(table.at[pl.ds(15, 3)], halo_y.at[1])
    along_x(15, 3)

    scale = 1.0 / math.sqrt(atoms_total * wave_vectors)
    loads[8].wait()
    factor = filt[...] * scale
    factor = jnp.concatenate([factor, factor], axis=0)
    mean_charge = total_charge / atoms_total
    plane_down = jnp.broadcast_to(plane, (8, 128)).T[:, 0:1]
    across_split = split(waves_across)
    around_split = split(waves_across - plane / atoms_total)
    sides = split(jnp.concatenate([grad_input, charges - mean_charge], axis=1))
    wait_bytes(summed.at[pl.ds(0, PEERS - 1)], recv_sem.at[2])
    filtered = factor * (summed[0:16].reshape(128, 128) - plane_down * mean_charge)
    filtered_response = factor * summed[16:32].reshape(128, 128)
    long_part = dot3(across_split, split(filtered))
    charge_part = dot3(around_split, split(filtered_response))

    part[:, 0:16, :] = long_part.reshape(GROUP, 16, 128)
    part[:, 16:32, :] = charge_part.reshape(GROUP, 16, 128)
    theirs = pl.ds(8 - core * 8, 8)

    def pair_up(first, count):
        pltpu.make_async_remote_copy(
            src_ref=part.at[theirs, pl.ds(first, count)],
            dst_ref=pair_in.at[:, pl.ds(first, count)],
            send_sem=send_sem.at[5],
            recv_sem=recv_sem.at[5],
            device_id=mate(SIBLING)[1],
            device_id_type=MESH,
        ).start()

    pair_up(0, 32)

    def swapped(values):
        return jnp.concatenate([values[64:], values[:64]], axis=0)

    both = jnp.concatenate([swapped(filtered), swapped(filtered_response)], axis=1)
    phase_grad = waves * dot3(split(both), sides, ((1,), (1,)))
    signed = jnp.where(iota((8, 128), 1) < 64, triples, -triples).astype(BF16)
    phase_high, phase_low = split(phase_grad)
    pgrad = (dot(signed, phase_high) + dot(signed, phase_low)) * (
        2.0 * math.pi / (cell_length * side)
    )
    for device in range(GROUP):
        low = 128 * (device // 8)
        values = pgrad[:, low : low + 128]
        if device % 8:
            values = pltpu.roll(values, 128 - 16 * (device % 8), axis=1)
        part[device, 32:40, :] = values

    pair_up(32, SENT - 32)
    wait_bytes(pair_in.at[:, pl.ds(0, SENT)], recv_sem.at[5])
    merged[:, 0:SENT, :] = part[ours, 0:SENT, :] + pair_in[:, 0:SENT, :]
    own = group % 8
    for bits in mates:
        other, device = mate(bits)
        pltpu.make_async_remote_copy(
            src_ref=merged.at[other % 8, pl.ds(0, SENT)],
            dst_ref=part_in.at[bits - 1, pl.ds(0, SENT)],
            send_sem=send_sem.at[3],
            recv_sem=recv_sem.at[3],
            device_id=device,
            device_id_type=MESH,
        ).start()

    wait_bytes(table.at[pl.ds(0, 9)], halo_x.at[0])
    wait_bytes(table.at[pl.ds(18, 9)], halo_x.at[1])
    collected = dot(mixers, table[...].reshape(512, 1280))

    def pair(first, lanes):
        return collected[first : first + 16, lanes] + collected[first + 16 : first + 32, lanes]

    loads[9].wait()
    mixed = dot(jnp.concatenate(split(pair(0, slice(0, 640))), axis=0), w0[...])
    mixed = mixed[0:16] + mixed[16:32]
    messages = {l * l + l: mixed[:, 128 * l : 128 * l + 128] for l in range(5)}
    for order, plus, minus, load, weights in (
        (1, pair(32, slice(640, 1152)), pair(64, slice(0, 512)), loads[10], w1),
        (2, pair(96, slice(512, 896)), pair(96, slice(896, 1280)), loads[11], w2),
    ):
        load.wait()
        wide = (5 - order) * 128
        product = dot(jnp.concatenate(split(plus) + split(minus), axis=0), weights[...])
        from_plus = product[0:16] + product[16:32]
        from_minus = product[32:48] + product[48:64]
        mixed_plus = from_plus[:, :wide] - from_minus[:, wide:]
        mixed_minus = from_minus[:, :wide] + from_plus[:, wide:]
        for at, degree in enumerate(range(order, 5)):
            center = degree * degree + degree
            messages[center + order] = mixed_plus[:, 128 * at : 128 * at + 128]
            messages[center - order] = mixed_minus[:, 128 * at : 128 * at + 128]
    for slot, message in messages.items():
        out_ref[slot] = (node_ref[slot].astype(F32) + message).astype(BF16)
    for slot in untouched:
        out_ref[slot] = node_ref[slot]

    stores = [
        pltpu.make_async_copy(source, target, store_sem.at[at])
        for at, (source, target) in enumerate(
            (
                (out_ref, out_hbm),
                (result_ref.at[pl.ds(0, 16)], long_hbm),
                (result_ref.at[pl.ds(16, 16)], charge_hbm),
                (pgrad_ref, pgrad_hbm),
            )
        )
    ]
    stores[0].start()

    all_parts = part_in.at[:, pl.ds(0, SENT), :]
    wait_bytes(all_parts, recv_sem.at[3])
    result = merged[own, 0:SENT, :] + jnp.sum(part_in[:, 0:SENT, :], axis=0)
    result_ref[0:32] = result[0:32]
    for axis in range(3):
        pgrad_ref[axis] = result[32 + axis : 33 + axis, 0:16]
    for store in stores[1:]:
        store.start()

    wait_bytes(table.at[pl.ds(0, 26)], halo_send)
    wait_bytes(all_parts, send_sem.at[0])
    wait_bytes(pair_in.at[:, pl.ds(0, SENT)], send_sem.at[4])
    wait_bytes(all_tiles, send_sem.at[1])
    wait_bytes(summed.at[pl.ds(0, PEERS - 1)], send_sem.at[2])
    wait_bytes(all_parts, send_sem.at[3])
    wait_bytes(pair_in.at[:, pl.ds(0, SENT)], send_sem.at[5])
    for store in stores:
        store.wait()


def settle(*refs):
    sources, targets, held, sems = refs[0:4], refs[4:8], refs[8:12], refs[12]
    pieces = [(0, pl.ds(5 * at, 5)) for at in range(5)] + [(at, slice(None)) for at in (1, 2, 3)]
    into = [
        pltpu.make_async_copy(sources[of].at[rows], held[of].at[rows], sems.at[at])
        for at, (of, rows) in enumerate(pieces)
    ]
    out = [
        pltpu.make_async_copy(held[of].at[rows], targets[of].at[rows], sems.at[8 + at])
        for at, (of, rows) in enumerate(pieces)
    ]
    for copy in into:
        copy.start()
    for arrive, leave in zip(into, out):
        arrive.wait()
        leave.start()
    for copy in out:
        copy.wait()


def local(
    node_irreps,
    positions,
    send_list,
    neighbours,
    displacements,
    order_zero,
    order_one,
    order_two,
    reciprocal_triples,
    reciprocal_filter,
    cotangent,
):
    far = pl.BlockSpec(memory_space=pl.ANY)
    results = (
        jax.ShapeDtypeStruct((25, 16, 128), BF16),
        jax.ShapeDtypeStruct((16, 128), F32),
        jax.ShapeDtypeStruct((16, 128), F32),
        jax.ShapeDtypeStruct((3, 1, 16), F32),
    )
    held = pl.pallas_call(
        kernel,
        out_shape=results,
        in_specs=[far] * 11,
        out_specs=(far,) * 4,
        scratch_shapes=[
            pltpu.VMEM((16, 128), BF16),
            pltpu.VMEM((25, 16, 128), BF16),
            pltpu.VMEM((3, 1, 16), F32),
            pltpu.VMEM((1, 8), jnp.int32),
            pltpu.VMEM((16, 32), jnp.int32),
            pltpu.VMEM((3, 1, 512), F32),
            pltpu.VMEM((640, 640), BF16),
            pltpu.VMEM((512, 1024), BF16),
            pltpu.VMEM((384, 768), BF16),
            pltpu.VMEM((3, 1024), jnp.int32),
            pltpu.VMEM((64, 128), F32),
            pltpu.VMEM((16, 128), F32),
            pltpu.VMEM((25, 16, 128), BF16),
            pltpu.VMEM((40, 128), F32),
            pltpu.VMEM((3, 1, 16), F32),
            pltpu.VMEM((32, 16, 1280), BF16),
            pltpu.VMEM((GROUP, 40, 128), F32),
            pltpu.VMEM((8, 128), F32),
            pltpu.VMEM((PEERS, 16, 128), F32),
            pltpu.VMEM((PEERS - 1, 16, 128), F32),
            pltpu.VMEM((PEERS, 8, 128), F32),
            pltpu.VMEM((GROUP, 40, 128), F32),
            pltpu.VMEM((8, 40, 128), F32),
            pltpu.VMEM((8, 40, 128), F32),
            pltpu.VMEM((7, 40, 128), F32),
            pltpu.SemaphoreType.DMA((12,)),
            pltpu.SemaphoreType.DMA((4,)),
            pltpu.SemaphoreType.DMA,
            pltpu.SemaphoreType.DMA((2,)),
            pltpu.SemaphoreType.DMA((2,)),
            pltpu.SemaphoreType.DMA((2,)),
            pltpu.SemaphoreType.DMA((6,)),
            pltpu.SemaphoreType.DMA((6,)),
            pltpu.SemaphoreType.REGULAR,
        ],
        compiler_params=pltpu.CompilerParams(
            collective_id=0, has_side_effects=True, vmem_limit_bytes=60 * 1024 * 1024
        ),
    )(
        jnp.transpose(node_irreps[0, 0, 0], (1, 0, 2)),
        positions.reshape(3, 1, 16),
        send_list.reshape(1, 8),
        neighbours.reshape(16, 32),
        displacements.reshape(3, 1, 512),
        order_zero,
        order_one,
        order_two,
        reciprocal_triples.T,
        reciprocal_filter,
        cotangent.reshape(16, 128),
    )
    updated, long_range, charge_grad, position_grad = pl.pallas_call(
        settle,
        out_shape=results,
        in_specs=[far] * 4,
        out_specs=(far,) * 4,
        scratch_shapes=[pltpu.VMEM(held_one.shape, held_one.dtype) for held_one in results]
        + [pltpu.SemaphoreType.DMA((16,))],
        compiler_params=pltpu.CompilerParams(vmem_limit_bytes=60 * 1024 * 1024),
    )(*held)
    return (
        jnp.transpose(updated, (1, 0, 2))[None, None, None],
        long_range[None, None, None],
        charge_grad[None, None, None],
        position_grad.reshape(1, 1, 1, 3, 16),
    )


def solution(mesh):
    by_block = ("gx", "gy", "gz")
    return jax.shard_map(
        local,
        mesh=mesh,
        in_specs=(
            P(*by_block, None, None, None),
            P(*by_block, None, None),
            P(*by_block, None),
            P(*by_block, None, None),
            P(*by_block, None, None),
            P(),
            P(),
            P(),
            P(),
            P(),
            P(*by_block, None, None),
        ),
        out_specs=(
            P(*by_block, None, None, None),
            P(*by_block, None, None),
            P(*by_block, None, None),
            P(*by_block, None, None),
        ),
        check_vma=False,
    )
```
